1024 devices in a mesh: dp: 64 (over z, y_lo), node: 16 (over y_hi, x, core).
Axes of the slice: x: 4, y: 4 (y_hi: 2, y_lo: 2; y = y_hi * 2 + y_lo), z: 32, core: 2. Of those that a mesh axis runs over, the one named last changes fastest.
Arguments:
- x_this: bfloat16 [64, 2048, 4096], P('dp', 'node'), may hold values from -6 to 6
- grad_values: bfloat16 [64, 2048, 512], P('dp', 'node'), may hold values from -0.046875 to 0.046875
- x_lower: bfloat16 [64, 2048, 4096], P('dp', 'node'), may hold values from -6 to 6
- norm_gain: float32 [4096], replicated, may hold values from 0.1 to 1.9
- weight_lower: bfloat16 [4096, 512], P('node'), may hold values from -0.09375 to 0.09375
- segment_ids: int32 [64, 2048], P('dp', 'node'), may hold values from 0 to 7, never falling along the last dimension, each value on 1 to 1024 neighbouring positions
Outputs:
- grad_weight: float32 [4096, 512], P('node', 'dp')
- keys_lower: bfloat16 [64, 2048, 512], P('dp', 'node')
The draws below stay inside these ranges and needn't reach their ends.
Inputs may be any that keep to these rules, and one draw needn't show every extreme that they name: `segment_ids`: document ids never fall along a sequence, start at 0, and each of the 8 documents holds 1 to 1024 tokens.
All inputs are finite; a program needn't handle non-finite values.
Results may differ from the reference program's by a relative error of at most 0.015.
Values may be sent and summed in bfloat16 or wider, within the bound.
A program may use at most 32 MiB of HBM per device.

```python
import math
import jax
import jax.numpy as jnp
import numpy as np
from jax import lax

DW = 4096
KV_HEADS = 4
HEAD_DIM = 128
DOCS = 8
TOK_DEV = 128
KW = 512
PACK = 2048
N_DP = 64
N_NODE = 16


def raised(entries, key, source, target, shards_of, factor):
    owner, partner = [(jnp.arange(entries.shape[axis_at]) // (entries.shape[axis_at] // shards_of)).reshape([-1 if axis == axis_at else 1 for axis in range(entries.ndim)]) for axis_at in (source, target)]
    chosen = jax.random.permutation(key, shards_of)[partner]
    strong = (owner == chosen) | (owner == (partner + shards_of // 2) % shards_of)
    return jnp.where(strong, factor * entries, entries)


def shard_levels(own_key, extent, split, low, largest):
    def one(position, blocks):
        heights = jax.random.uniform(jax.random.fold_in(jax.random.fold_in(own_key, 6), position), (blocks,), jnp.float32, low / len(split), largest / len(split))
        return jnp.repeat(jnp.exp(heights), extent[position] // blocks).reshape((-1,) + (1,) * (len(extent) - position - 1))

    level = one(*split[0])
    for cut in split[1:]:
        level = level * one(*cut)
    return level


def split_up(amount, total, bound, slope):
    loads = [(1 << 20) // math.isqrt(rank ** slope) + 1 for rank in range(2, amount + 1)]
    spare, holding = total - bound - (amount - 1), [1] * (amount - 1)
    while spare > 0:
        free = [i for i in range(amount - 1) if holding[i] < bound]
        mass, remaining = sum([loads[i] for i in free]), spare
        for i in free:
            more = min(bound - holding[i], max(1, remaining * loads[i] // mass), spare)
            holding[i] = holding[i] + more
            spare = spare - more
    return np.array([bound] + holding)


def uneven_parts(rng, number_of, total, most, lean):
    if number_of == 2:
        one = jax.random.randint(rng, (), max(1, total - most), min(most, total - 1) + 1)
        return jnp.stack([one, total - one])
    lengths = jnp.asarray(split_up(number_of, total, most, lean), jnp.int32)
    pairs = (number_of - 1) // 2
    giver, receiver = lengths[1:1 + 2 * pairs:2], lengths[2:2 + 2 * pairs:2]
    room = jnp.minimum(giver - 1, most - receiver)
    moved = jax.random.randint(jax.random.fold_in(rng, 1), (pairs,), 0, 1 << 20) % (room + 1)
    lengths = lengths.at[1:1 + 2 * pairs:2].set(giver - moved).at[2:2 + 2 * pairs:2].set(receiver + moved)
    return lengths[jax.random.permutation(jax.random.fold_in(rng, 2), number_of)]


def scatter_about(key, dims, scale, limit, cuts=(), kind=jnp.bfloat16):
    result = jax.random.normal(key, dims, jnp.float32) * scale
    if len(cuts) > 0:
        result = shard_levels(key, dims, cuts, -0.22, 0.18) * result
    return jnp.clip(result, min=-limit, max=limit).astype(kind)


def heavy_noise(own_key, dims, spread, most, pieces, heavy, kind=jnp.bfloat16):
    entries = spread * jax.random.normal(own_key, dims, jnp.float32)
    if pieces:
        entries = entries * shard_levels(own_key, dims, pieces, -0.22, 0.18)
    return jnp.clip(raised(entries, jax.random.fold_in(own_key, 3), *heavy), -most, most).astype(kind)


def setup_inputs(seed: int = 0) -> dict:
    streams_of = jax.random.split(jax.random.key(seed), 7)
    x_this = heavy_noise(streams_of[0], (N_DP, PACK, DW), 1.0, 6.0, ((0, 64), (1, 16)), (1, 2, 16, 2.0))
    grad_values = heavy_noise(streams_of[1], (N_DP, PACK, KW), ((PACK * N_DP) ** -0.5), 0.046875, ((0, 64), (1, 16)), (0, 2, 64, 4.0))
    x_lower = scatter_about(streams_of[2], (N_DP, PACK, DW), 1.0, 6.0, ((0, 64), (1, 16)))
    norm_gain = jnp.clip(1.0 + 0.18 * jax.random.normal(streams_of[3], (DW,), jnp.float32), 0.1, 1.9)
    weight_lower = scatter_about(streams_of[4], (DW, KW), DW ** -0.5, 0.09375, ((0, 16),))
    segment_ids = jax.vmap(lambda own: jnp.searchsorted(jnp.cumsum(uneven_parts(own, DOCS, PACK, PACK // 2, 1)), jnp.arange(PACK), side="right"))(jax.random.split(streams_of[5], N_DP)).reshape((N_DP, PACK)).astype(jnp.int32)
    return dict(x_this=x_this, grad_values=grad_values, x_lower=x_lower, norm_gain=norm_gain, weight_lower=weight_lower, segment_ids=segment_ids)


epsilon = 1e-05

def rotate_keys(raw_keys, positions):
    half_size = HEAD_DIM // 2
    heads = raw_keys.reshape(raw_keys.shape[0], KV_HEADS, HEAD_DIM)
    frequency = 500000.0 ** (-(jnp.arange(half_size, dtype=jnp.float32) * 2.0 / HEAD_DIM))
    angle = positions.astype(jnp.float32)[:, None] * frequency[None, :]
    cosine = jnp.cos(angle)[:, None, :]
    sine = jnp.sin(angle)[:, None, :]
    first_half = heads[:, :, :half_size]
    second_half = heads[:, :, half_size:]
    turned = jnp.concatenate([first_half * cosine - second_half * sine, second_half * cosine + first_half * sine], axis=2)
    return turned.reshape(raw_keys.shape[0], KW)

def one_sequence(pair, norm_gain, weight_lower):
    inputs_row, doc_ids = pair
    lower_f32 = inputs_row.astype(jnp.float32)
    mean_sq = lax.optimization_barrier(jnp.mean(lower_f32 * lower_f32, axis=1, keepdims=True))
    normed = (lower_f32 * lax.rsqrt(mean_sq + epsilon) * norm_gain[None, :]).astype(jnp.bfloat16)
    raw_keys = jnp.dot(normed, weight_lower, preferred_element_type=jnp.float32)
    steps_here = jnp.arange(PACK, dtype=jnp.int32)
    before_ids = jnp.concatenate([doc_ids[:1], doc_ids[:-1]])
    marks = jnp.where(doc_ids != before_ids, steps_here, jnp.int32(0))
    positions = steps_here - lax.cummax(marks, axis=0)
    return rotate_keys(raw_keys, positions).astype(jnp.bfloat16)

def reference(x_this, grad_values, x_lower, norm_gain, weight_lower, segment_ids):
    blocks_x = x_this.reshape(N_DP * N_NODE, TOK_DEV, DW)
    blocks_g = grad_values.reshape(N_DP * N_NODE, TOK_DEV, KW)

    def add_block(running, blocks):
        grad_term = lax.dot_general(blocks[0], blocks[1], (((0,), (0,)), ((), ())), preferred_element_type=jnp.float32)
        rounded = lax.optimization_barrier(grad_term.astype(jnp.bfloat16))
        return (running + rounded.astype(jnp.float32), None)
    grad_weight, unused = lax.scan(add_block, jnp.zeros((DW, KW), jnp.float32), (blocks_x, blocks_g))
    keys_lower = lax.map(lambda pair: one_sequence(pair, norm_gain, weight_lower), (x_lower, segment_ids))
    return (grad_weight, keys_lower)
```

```python
import functools
import math

import jax
import jax.numpy as jnp
import numpy as np
from jax import lax
from jax.experimental import pallas as pl
from jax.experimental.pallas import tpu as pltpu
from jax.sharding import PartitionSpec as P

EPS = 1e-05
MESH = pl.DeviceIdType.MESH
F32 = jnp.float32
BF16 = jnp.bfloat16
N_SEM = 72
ORDER = (2, 1, 3, 0)
ROUTES = (("x", 1, 3), ("x", 3, 1), ("y", 1, 3), ("y", 3, 1))


def flip(v, mask):
    if mask == 0:
        return v
    if mask == 1:
        return v + 1 - 2 * lax.rem(v, 2)
    if mask == 2:
        return lax.rem(v + 2, 4)
    return 3 - v


def kernel(
    x_hbm, g_hbm, low_hbm, gain_hbm, w_hbm, ids_hbm, freq_hbm,
    grad_ref, keys_ref,
    x_v, g_v, low_v, gain_v, w_v, ids_v, freq_v,
    gt_f, gt2, c_send, c_recv, s_buf, r1, r2, r3, r4, z1, z2, zs,
    wg, normed, acc, kr, cs, cr,
    local_sem, send_sem, recv_sem,
):
    dp = lax.axis_index("dp")
    node = lax.axis_index("node")
    z, yl = lax.div(dp, 2), lax.rem(dp, 2)
    yh = lax.div(node, 8)
    x = lax.rem(lax.div(node, 2), 4)
    c = lax.rem(node, 2)
    y = yh * 2 + yl
    par = lax.rem(z, 2)

    def dev(jx=0, jy=0, dz=0, other=False):
        ty = flip(y, jy)
        tz = lax.rem(z + dz + 32, 32)
        tc = 1 - c if other else c
        return (tz * 2 + lax.rem(ty, 2), lax.div(ty, 2) * 8 + flip(x, jx) * 2 + tc)

    sent = []

    def send(src, dst, device):
        i = len(sent)
        copy = pltpu.make_async_remote_copy(
            src_ref=src, dst_ref=dst, send_sem=send_sem.at[i], recv_sem=recv_sem.at[i],
            device_id=device, device_id_type=MESH,
        )
        copy.start()
        sent.append(copy)
        return copy

    loads = []
    for src, dst in (
        (g_hbm, g_v), (x_hbm, x_v), (w_hbm, w_v), (ids_hbm, ids_v),
        (low_hbm, low_v), (gain_hbm, gain_v), (freq_hbm, freq_v),
    ):
        copy = pltpu.make_async_copy(src, dst, local_sem.at[len(loads)])
        copy.start()
        loads.append(copy)
    ld_g, ld_x, ld_w, ld_ids, ld_low, ld_gain, ld_freq = loads

    barrier = pltpu.get_barrier_semaphore()
    greet = [dev(other=True), dev(jx=1), dev(jx=3), dev(jy=1), dev(jy=3), dev(jy=2)]
    greet += [dev(dz=1), dev(dz=-1), dev(dz=2), dev(dz=-2)]
    greet += [dev(dz=4 * a) for a in range(1, 8)]
    for device in greet:
        pl.semaphore_signal(barrier, inc=1, device_id=device, device_id_type=MESH)

    ld_g.wait()
    gt_f[...] = g_v[0].astype(F32).T.reshape(32, 2, 8, 128)
    mine_first = jnp.concatenate([gt_f[:, yl], gt_f[:, 1 - yl]], axis=1).astype(BF16).reshape(512, 128)
    gt2[0:512, :] = mine_first
    gt2[512:1024, :] = mine_first
    g_rows = pl.ds(pl.multiple_of(z * 16, 16), 512)

    def term(jx, jyh, core):
        owner = (yh + jyh - 2 * yh * jyh) * 8 + flip(x, jx) * 2 + core
        lanes = pl.ds(pl.multiple_of(owner * 256, 256), 256)
        t = jnp.dot(gt2[g_rows, :], x_v[0, :, lanes], preferred_element_type=F32)
        t = t.reshape(8, 4, 2, 8, 256)

        def piece(b, jl):
            part = t[:, b, jl]
            return jnp.concatenate([part[:, :, :128], part[:, :, 128:]], axis=1)

        return piece

    ld_x.wait()
    ld_ids.wait()
    ids_row = jnp.broadcast_to(ids_v[...].astype(F32), (128, 128))
    sub = lax.broadcasted_iota(jnp.int32, (128, 128), 0)
    lane = lax.broadcasted_iota(jnp.int32, (128, 128), 1)
    id_col = jnp.sum(jnp.where(sub == lane, ids_row, 0.0), axis=1, keepdims=True)
    lane_f = lane.astype(F32)
    count = jnp.sum(jnp.where(id_col < lane_f, 1.0, 0.0), axis=0, keepdims=True)
    cs[0] = jnp.broadcast_to(count, (8, 128))

    c_copies = {}
    w0 = None
    for step, jx in enumerate(ORDER):
        for jyh in range(2):
            piece = term(jx, jyh, 1 - c)
            for b in range(4):
                for jl in range(2):
                    c_send[jx, jyh, b, jl] = piece(b, jl).astype(BF16)
            if step == 0 and jyh == 0:
                pl.semaphore_wait(barrier, len(greet))
                cc = [send(cs.at[0], cr.at[0], dev(other=True))]
                ld_w.wait()
                rows = pl.ds(pl.multiple_of(par * 128, 128), 128)
                away = pl.ds(pl.multiple_of((1 - c) * 256, 256), 256)
                here = pl.ds(pl.multiple_of(c * 256, 256), 256)
                wg[0, 0, 0, c] = w_v[rows, here]
                kr_w = w_v.at[rows, away]
                w0 = send(kr_w, wg.at[0, 0, 0, c], dev(other=True))
            c_copies[jx, jyh] = send(c_send.at[jx, jyh], c_recv.at[jx, jyh], dev(other=True))

    w0.wait_recv()
    w1a = send(wg.at[0, 0, 0], wg.at[0, 0, 1], dev(jx=1))
    w1b = send(wg.at[0, 0, 0], wg.at[0, 0, 3], dev(jx=3))

    r1_copies = {b: [] for b in range(4)}
    for jx in ORDER:
        for jyh in range(2):
            piece = term(jx, jyh, c)
            c_copies[jx, jyh].wait_recv()
            for b in range(4):
                for jl in range(2):
                    jy = jyh * 2 + jl
                    total = (piece(b, jl) + c_recv[jx, jyh, b, jl].astype(F32)).astype(BF16)
                    if b < 2:
                        s_buf[b, jx, jy] = total
                    else:
                        s_buf[b, jy, jx] = total
        for b, (axis, m1, m2) in enumerate(ROUTES):
            low = min(m1, 2)
            if axis == "x":
                if jx in (m1, 2):
                    r1_copies[b].append(send(s_buf.at[b, jx], r1.at[b, jx - low], dev(jx=m1)))
            else:
                r1_copies[b].append(
                    send(s_buf.at[b, low:low + 2, jx], r1.at[b, :, jx], dev(jy=m1))
                )

    cc[0].wait_recv()
    cs[1] = cs[0] + cr[0]
    cc.append(send(cs.at[1], cr.at[1], dev(jx=1)))

    w1a.wait_recv()
    w1b.wait_recv()
    w2a = send(wg.at[0, 0, 3, 0], wg.at[0, 0, 2, 0], dev(jx=1))
    w2b = send(wg.at[0, 0, 1, 1], wg.at[0, 0, 2, 1], dev(jx=3))

    ld_low.wait()
    ld_gain.wait()
    gain = gain_v[...]

    def norm_rows(i, carry):
        rows = pl.ds(pl.multiple_of(i * 16, 16), 16)
        v = low_v[0, rows, :].astype(F32)
        mean_sq = jnp.sum(v * v, axis=1, keepdims=True) * (1.0 / 4096)
        normed[rows, :] = (v * lax.rsqrt(mean_sq + EPS) * gain).astype(BF16)
        return carry

    lax.fori_loop(0, 8, norm_rows, 0)
    nb = send(normed.at[0:128], normed.at[128:256], dev(other=True))

    w2a.wait_recv()
    w2b.wait_recv()
    w3 = send(wg.at[0, 0, :, 1 - yl], wg.at[0, 1, :, 1 - yl], dev(jy=3))
    w5 = [
        send(wg.at[0, 0, :, 0], wg.at[1, 0, :, 0], dev(dz=1)),
        send(wg.at[0, 0, :, 1], wg.at[1, 0, :, 1], dev(dz=-1)),
    ]

    cc[1].wait_recv()
    cs[2] = cs[1] + cr[1]
    cc.append(send(cs.at[2], cr.at[2], dev(jx=3)))

    def to(axis, mask):
        return dev(jx=mask) if axis == "x" else dev(jy=mask)

    r2_copies = []
    for b, (axis, m1, m2) in enumerate(ROUTES):
        for copy in r1_copies[b]:
            copy.wait_recv()
        low = min(m1, 2)
        s_buf[b, m2] = s_buf[b, m2] + r1[b, 2 - low]
        r2_copies.append(send(s_buf.at[b, m2], r2.at[b], to(axis, m2)))
        s_buf[b, 0] = s_buf[b, 0] + r1[b, m1 - low]

    w3.wait_recv()
    w4 = send(wg.at[0, 1, :, yl], wg.at[0, 1, :, yl], dev(jy=1))
    w5.append(send(wg.at[0, 1, :, yl], wg.at[1, 1, :, yl], dev(dz=1 - 2 * yl)))

    r3_copies = []
    for b, (axis, m1, m2) in enumerate(ROUTES):
        r2_copies[b].wait_recv()
        other = "y" if axis == "x" else "x"
        low = min(m1, 2)
        s_buf[b, 0] = s_buf[b, 0] + r2[b]
        r3_copies.append(send(s_buf.at[b, 0, low:low + 2], r3.at[b], to(other, m1)))

    cc[2].wait_recv()
    cs[3] = cs[2] + cr[2]
    cc.append(send(cs.at[3], cr.at[3], dev(jy=2)))

    r4_copies = []
    for b, (axis, m1, m2) in enumerate(ROUTES):
        r3_copies[b].wait_recv()
        other = "y" if axis == "x" else "x"
        low = min(m1, 2)
        s_buf[b, 0, m2] = s_buf[b, 0, m2] + r3[b, 2 - low]
        r4_copies.append(send(s_buf.at[b, 0, m2], r4.at[b], to(other, m2)))
        s_buf[b, 0, 0] = s_buf[b, 0, 0] + r3[b, m1 - low]

    w4.wait_recv()
    w5.append(send(wg.at[0, 1, :, 1 - yl], wg.at[1, 1, :, 1 - yl], dev(dz=2 * yl - 1)))

    z1_copies = []
    for b in (1, 2, 3):
        r4_copies[b].wait_recv()
        s_buf[b, 0, 0] = s_buf[b, 0, 0] + r4[b]
        z1_copies.append(send(s_buf.at[b, 0, 0], z1.at[b - 1], dev(dz=(0, 1, 2, -1)[b])))
    r4_copies[0].wait_recv()
    kept = s_buf[0, 0, 0].astype(F32) + r4[0].astype(F32)

    nb.wait_recv()

    def project(jp):
        for jyh in range(2):
            for jx in range(4):
                owner = (yh + jyh - 2 * yh * jyh) * 8 + flip(x, jx) * 2
                half = par if jp == 0 else 1 - par
                lhs = jnp.concatenate(
                    [
                        normed[:, pl.ds(pl.multiple_of((owner + s) * 256 + half * 128, 128), 128)]
                        for s in range(2)
                    ],
                    axis=1,
                )
                part = jnp.dot(lhs, wg[jp, jyh, jx].reshape(256, 256), preferred_element_type=F32)
                if jp == 0 and jyh == 0 and jx == 0:
                    acc[...] = part
                else:
                    acc[...] += part

    project(0)

    for copy in z1_copies:
        copy.wait_recv()
    kept = kept + z1[0].astype(F32) + z1[1].astype(F32)
    late = z1[2].astype(F32)
    kept = kept + jnp.concatenate([late[7:8], late[0:7]], axis=0)
    zs[...] = kept.astype(BF16)
    z2_copies = [send(zs.at[a], z2.at[a - 1], dev(dz=4 * a)) for a in range(1, 8)]

    for copy in w5:
        copy.wait_recv()
    project(1)
    kx = send(acc.at[128:256], kr, dev(other=True))

    cc[3].wait_recv()
    counts = (cs[3] + cr[3])[0:1]
    start = jnp.sum(jnp.where(lane_f == id_col, counts, 0.0), axis=1, keepdims=True)
    first_token = (node * 128).astype(F32)
    token = lax.broadcasted_iota(jnp.int32, (128, 1), 0).astype(F32)
    positions = token + first_token - start
    ld_freq.wait()
    angle = positions * freq_v[...]
    cosine = jnp.cos(angle)
    sine = jnp.where(lane < 64, -1.0, 1.0) * jnp.sin(angle)

    def rotate(source, half):
        for h in range(2):
            k = source[0:128, h * 128:(h + 1) * 128]
            turned = k * cosine + pltpu.roll(k, 64, 1) * sine
            lanes = pl.ds(pl.multiple_of(half * 256 + h * 128, 128), 128)
            keys_ref[:, lanes] = turned.astype(BF16)

    rotate(acc, c)
    kx.wait_recv()
    rotate(kr, 1 - c)

    total = kept[0]
    for a in range(7):
        z2_copies[a].wait_recv()
        total = total + z2[a].astype(F32)
    grad_ref[...] = total

    for copy in sent:
        copy.wait_send()


def fused(x_this, grad_values, x_lower, gain, weight_lower, ids, freq):
    tiles = (8, 16, 128)
    anywhere = pl.BlockSpec(memory_space=pl.ANY)
    vmem = pl.BlockSpec(memory_space=pltpu.VMEM)
    return pl.pallas_call(
        kernel,
        out_shape=(
            jax.ShapeDtypeStruct((16, 128), F32),
            jax.ShapeDtypeStruct((128, 512), BF16),
        ),
        in_specs=[anywhere] * 7,
        out_specs=(vmem, vmem),
        scratch_shapes=[
            pltpu.VMEM((1, 128, 4096), BF16),
            pltpu.VMEM((1, 128, 512), BF16),
            pltpu.VMEM((1, 128, 4096), BF16),
            pltpu.VMEM((1, 4096), F32),
            pltpu.VMEM((256, 512), BF16),
            pltpu.VMEM((1, 128), jnp.int32),
            pltpu.VMEM((1, 128), F32),
            pltpu.VMEM((32, 2, 8, 128), F32),
            pltpu.VMEM((1024, 128), BF16),
            pltpu.VMEM((4, 2, 4, 2) + tiles, BF16),
            pltpu.VMEM((4, 2, 4, 2) + tiles, BF16),
            pltpu.VMEM((4, 4, 4) + tiles, BF16),
            pltpu.VMEM((4, 2, 4) + tiles, BF16),
            pltpu.VMEM((4, 4) + tiles, BF16),
            pltpu.VMEM((4, 2) + tiles, BF16),
            pltpu.VMEM((4,) + tiles, BF16),
            pltpu.VMEM((3,) + tiles, BF16),
            pltpu.VMEM((7, 16, 128), BF16),
            pltpu.VMEM(tiles, BF16),
            pltpu.VMEM((2, 2, 4, 2, 128, 256), BF16),
            pltpu.VMEM((256, 4096), BF16),
            pltpu.VMEM((256, 256), F32),
            pltpu.VMEM((128, 256), F32),
            pltpu.VMEM((4, 8, 128), F32),
            pltpu.VMEM((4, 8, 128), F32),
            pltpu.SemaphoreType.DMA((7,)),
            pltpu.SemaphoreType.DMA((N_SEM,)),
            pltpu.SemaphoreType.DMA((N_SEM,)),
        ],
        compiler_params=pltpu.CompilerParams(
            collective_id=0, has_side_effects=True, vmem_limit_bytes=40 * 1024 * 1024
        ),
        cost_estimate=pl.CostEstimate(
            flops=2 * 2 * 128 * 4096 * 512, bytes_accessed=4 * 1024 * 1024, transcendentals=32768
        ),
    )(x_this, grad_values, x_lower, gain, weight_lower, ids, freq)


def on_device(x_this, grad_values, x_lower, norm_gain, weight_lower, segment_ids):
    exponent = np.arange(128) % 64 * 2.0 / 128
    freq = jnp.asarray((500000.0 ** (-exponent)).astype(np.float32)[None])
    grad, keys = fused(
        x_this, grad_values, x_lower, norm_gain[None], weight_lower, segment_ids, freq
    )
    grad = grad.reshape(2, 8, 128).transpose(0, 2, 1).reshape(256, 8)
    return (grad, keys[None])


def solution(mesh):
    return jax.shard_map(
        on_device,
        mesh=mesh,
        in_specs=(
            P("dp", "node", None),
            P("dp", "node", None),
            P("dp", "node", None),
            P(),
            P("node", None),
            P("dp", "node"),
        ),
        out_specs=(P("node", "dp"), P("dp", "node", None)),
        check_vma=False,
    )
```

```python
import functools
import math

import jax
import jax.numpy as jnp
import numpy as np
from jax import lax
from jax.experimental import pallas as pl
from jax.experimental.pallas import tpu as pltpu
from jax.sharding import PartitionSpec as P

EPS = 1e-05
MESH = pl.DeviceIdType.MESH
F32 = jnp.float32
BF16 = jnp.bfloat16
N_SEM = 112
ORDER = (2, 1, 3, 0)
ROUTES = (("x", 1, 3), ("x", 3, 1), ("y", 1, 3), ("y", 3, 1))


def flip(v, mask):
    if mask == 0:
        return v
    if mask == 1:
        return v + 1 - 2 * lax.rem(v, 2)
    if mask == 2:
        return lax.rem(v + 2, 4)
    return 3 - v


def kernel(
    x_hbm, g_hbm, low_hbm, gain_hbm, w_hbm, ids_hbm, freq_hbm,
    grad_ref, keys_ref,
    x_v, g_v, low_v, gain_v, w_v, ids_v, freq_v,
    gt_f, gt2, c_send, c_recv, s_buf, r1, r2, r3, r4, z1, z2, zs,
    wg, normed, acc, kr, cs, cr, trig,
    local_sem, send_sem, recv_sem, far_sem,
):
    dp = lax.axis_index("dp")
    node = lax.axis_index("node")
    z, yl = lax.div(dp, 2), lax.rem(dp, 2)
    yh = lax.div(node, 8)
    x = lax.rem(lax.div(node, 2), 4)
    c = lax.rem(node, 2)
    y = yh * 2 + yl
    par = lax.rem(z, 2)

    def dev(jx=0, jy=0, dz=0, other=False):
        ty = flip(y, jy)
        tz = lax.rem(z + dz + 32, 32)
        tc = 1 - c if other else c
        return (tz * 2 + lax.rem(ty, 2), lax.div(ty, 2) * 8 + flip(x, jx) * 2 + tc)

    sent = []

    def send(src, dst, device):
        i = len(sent)
        copy = pltpu.make_async_remote_copy(
            src_ref=src, dst_ref=dst, send_sem=send_sem.at[i], recv_sem=recv_sem.at[i],
            device_id=device, device_id_type=MESH,
        )
        copy.start()
        sent.append(copy)
        return copy

    loads = []
    for src, dst in (
        (ids_hbm, ids_v), (g_hbm, g_v), (w_hbm, w_v), (x_hbm, x_v),
        (low_hbm, low_v), (gain_hbm, gain_v), (freq_hbm, freq_v),
    ):
        copy = pltpu.make_async_copy(src, dst, local_sem.at[len(loads)])
        copy.start()
        loads.append(copy)
    ld_ids, ld_g, ld_w, ld_x, ld_low, ld_gain, ld_freq = loads

    barrier = pltpu.get_barrier_semaphore()
    greet = [dev(other=True), dev(jx=1), dev(jx=3), dev(jy=1), dev(jy=3), dev(jy=2)]
    greet += [dev(dz=1), dev(dz=-1), dev(dz=2), dev(dz=-2)]
    for device in greet:
        pl.semaphore_signal(barrier, inc=1, device_id=device, device_id_type=MESH)

    ld_ids.wait()
    ids_row = jnp.broadcast_to(ids_v[...].astype(F32), (128, 128))
    sub = lax.broadcasted_iota(jnp.int32, (128, 128), 0)
    lane = lax.broadcasted_iota(jnp.int32, (128, 128), 1)
    id_col = jnp.sum(jnp.where(sub == lane, ids_row, 0.0), axis=1, keepdims=True)
    lane_f = lane.astype(F32)
    count = jnp.sum(jnp.where(id_col < lane_f, 1.0, 0.0), axis=0, keepdims=True)
    cs[0] = jnp.broadcast_to(count, (8, 128))

    ld_g.wait()
    gt_f[...] = g_v[0].astype(F32).T.reshape(32, 2, 8, 128)
    mine_first = jnp.concatenate([gt_f[:, yl], gt_f[:, 1 - yl]], axis=1).astype(BF16).reshape(512, 128)
    gt2[0:512, :] = mine_first
    gt2[512:1024, :] = mine_first
    g_rows = pl.ds(pl.multiple_of(z * 16, 16), 512)

    def term(jx, jyh, core):
        owner = (yh + jyh - 2 * yh * jyh) * 8 + flip(x, jx) * 2 + core
        lanes = pl.ds(pl.multiple_of(owner * 256, 256), 256)
        t = jnp.dot(gt2[g_rows, :], x_v[0, :, lanes], preferred_element_type=F32)
        t = t.reshape(8, 4, 2, 8, 256)

        def piece(b, jl):
            part = t[:, b, jl]
            return jnp.concatenate([part[:, :, :128], part[:, :, 128:]], axis=1)

        return piece

    ld_w.wait()
    rows = pl.ds(pl.multiple_of(par * 128, 128), 128)
    away = pl.ds(pl.multiple_of((1 - c) * 256, 256), 256)
    here = pl.ds(pl.multiple_of(c * 256, 256), 256)
    wg[0, 0, 0, c] = w_v[rows, here]
    pl.semaphore_wait(barrier, len(greet))
    def far_signal(i):
        for side in (1, -1):
            pl.semaphore_signal(
                far_sem.at[i], inc=1, device_id=dev(dz=side * 2 * 2 ** i), device_id_type=MESH
            )

    far_signal(0)
    w0 = send(w_v.at[rows, away], wg.at[0, 0, 0, c], dev(other=True))
    cc = [send(cs.at[0], cr.at[0], dev(other=True))]
    w3, w4, w5 = {}, {}, []

    def spread(jx):
        w3[jx] = send(wg.at[0, 0, jx, 1 - yl], wg.at[0, 1, jx, 1 - yl], dev(jy=3))
        w5.append(send(wg.at[0, 0, jx, 0], wg.at[1, 0, jx, 0], dev(dz=1)))
        w5.append(send(wg.at[0, 0, jx, 1], wg.at[1, 0, jx, 1], dev(dz=-1)))

    def share(jx):
        w3[jx].wait_recv()
        w4[jx] = send(wg.at[0, 1, jx, yl], wg.at[0, 1, jx, yl], dev(jy=1))
        w5.append(send(wg.at[0, 1, jx, yl], wg.at[1, 1, jx, yl], dev(dz=1 - 2 * yl)))

    def pass_on(jx):
        w4[jx].wait_recv()
        w5.append(send(wg.at[0, 1, jx, 1 - yl], wg.at[1, 1, jx, 1 - yl], dev(dz=2 * yl - 1)))

    ld_x.wait()
    c_copies = {}
    r1_copies = {}

    def for_sibling(jx):
        for jyh in (1, 0):
            piece = term(jx, jyh, 1 - c)
            for b in range(4):
                for jl in range(2):
                    c_send[jx, jyh, b, jl] = piece(b, jl).astype(BF16)
            c_copies[jx, jyh] = send(c_send.at[jx, jyh], c_recv.at[jx, jyh], dev(other=True))

    def own(jx):
        for jyh in (1, 0):
            piece = term(jx, jyh, c)
            c_copies[jx, jyh].wait_recv()
            for b in range(4):
                for jl in range(2):
                    jy = jyh * 2 + jl
                    total = (piece(b, jl) + c_recv[jx, jyh, b, jl].astype(F32)).astype(BF16)
                    if b < 2:
                        s_buf[b, jx, jy] = total
                    else:
                        s_buf[b, jy, jx] = total
            pair = slice(jyh * 2, jyh * 2 + 2)
            for b, (axis, m1, m2) in enumerate(ROUTES):
                low = min(m1, 2)
                if axis == "x" and jx in (m1, 2):
                    r1_copies[b, jx, jyh] = send(
                        s_buf.at[b, jx, pair], r1.at[b, jx - low, pair], dev(jx=m1)
                    )
        for b, (axis, m1, m2) in enumerate(ROUTES):
            low = min(m1, 2)
            if axis == "y":
                r1_copies[b, jx] = send(
                    s_buf.at[b, low:low + 2, jx], r1.at[b, :, jx], dev(jy=m1)
                )

    for_sibling(2)
    for_sibling(1)
    w0.wait_recv()
    w1a = send(wg.at[0, 0, 0], wg.at[0, 0, 1], dev(jx=1))
    w1b = send(wg.at[0, 0, 0], wg.at[0, 0, 3], dev(jx=3))
    spread(0)
    own(2)
    for_sibling(3)
    own(1)
    cc[0].wait_recv()
    cs[1] = cs[0] + cr[0]
    cc.append(send(cs.at[1], cr.at[1], dev(jx=1)))
    w1a.wait_recv()
    w1b.wait_recv()
    w2a = send(wg.at[0, 0, 3, 0], wg.at[0, 0, 2, 0], dev(jx=1))
    w2b = send(wg.at[0, 0, 1, 1], wg.at[0, 0, 2, 1], dev(jx=3))
    spread(1)
    spread(3)
    for_sibling(0)
    own(3)
    share(0)
    pl.semaphore_wait(far_sem.at[0], 2)
    far_signal(1)
    own(0)
    cc[1].wait_recv()
    cs[2] = cs[1] + cr[1]
    cc.append(send(cs.at[2], cr.at[2], dev(jx=3)))
    w2a.wait_recv()
    w2b.wait_recv()
    spread(2)
    share(1)
    pass_on(0)
    share(3)

    ld_low.wait()
    ld_gain.wait()
    gain = gain_v[...]

    def norm_rows(i, carry):
        rows = pl.ds(pl.multiple_of(i * 16, 16), 16)
        v = low_v[0, rows, :].astype(F32)
        mean_sq = jnp.sum(v * v, axis=1, keepdims=True) * (1.0 / 4096)
        normed[rows, :] = (v * lax.rsqrt(mean_sq + EPS) * gain).astype(BF16)
        return carry

    lax.fori_loop(0, 2, norm_rows, 0)

    def to(axis, mask):
        return dev(jx=mask) if axis == "x" else dev(jy=mask)

    r2_copies = {}
    for jx in ORDER:
        for b, (axis, m1, m2) in enumerate(ROUTES):
            low = min(m1, 2)
            if axis == "x":
                if jx not in (m1, 2):
                    continue
                slot = m2 if jx == 2 else 0
                for jyh in (1, 0):
                    pair = slice(jyh * 2, jyh * 2 + 2)
                    r1_copies[b, jx, jyh].wait_recv()
                    s_buf[b, slot, pair] = s_buf[b, slot, pair] + r1[b, jx - low, pair]
                    if slot:
                        r2_copies[b, jyh] = send(
                            s_buf.at[b, m2, pair], r2.at[b, pair], to(axis, m2)
                        )
            else:
                r1_copies[b, jx].wait_recv()
                s_buf[b, m2, jx] = s_buf[b, m2, jx] + r1[b, 2 - low, jx]
                r2_copies[b, jx] = send(s_buf.at[b, m2, jx], r2.at[b, jx], to(axis, m2))
                s_buf[b, 0, jx] = s_buf[b, 0, jx] + r1[b, m1 - low, jx]

    cc[2].wait_recv()
    cs[3] = cs[2] + cr[2]
    cc.append(send(cs.at[3], cr.at[3], dev(jy=2)))
    share(2)
    pass_on(1)
    pass_on(3)
    pl.semaphore_wait(far_sem.at[1], 2)
    far_signal(2)
    lax.fori_loop(2, 5, norm_rows, 0)

    r3_copies = {}

    def forward(b, s, other, m1):
        s_buf[b, 0, s] = s_buf[b, 0, s] + r2[b, s]
        if s in (m1, 2):
            r3_copies[b, s] = send(s_buf.at[b, 0, s], r3.at[b, s - min(m1, 2)], to(other, m1))

    for jx in ORDER:
        for b, (axis, m1, m2) in enumerate(ROUTES):
            if axis == "y":
                r2_copies[b, jx].wait_recv()
                forward(b, jx, "x", m1)
            elif jx in (2, 1):
                jyh = jx - 1
                r2_copies[b, jyh].wait_recv()
                for s in (2, 3) if jyh else (1, 0):
                    forward(b, s, "y", m1)

    pass_on(2)
    lax.fori_loop(5, 8, norm_rows, 0)
    nb = send(normed.at[0:128], normed.at[128:256], dev(other=True))

    cc[3].wait_recv()
    counts = (cs[3] + cr[3])[0:1]
    start = jnp.sum(jnp.where(lane_f == id_col, counts, 0.0), axis=1, keepdims=True)
    first_token = (node * 128).astype(F32)
    token = lax.broadcasted_iota(jnp.int32, (128, 1), 0).astype(F32)
    positions = token + first_token - start
    ld_freq.wait()
    angle = positions * freq_v[...]
    trig[0] = jnp.cos(angle)
    trig[1] = jnp.where(lane < 64, -1.0, 1.0) * jnp.sin(angle)

    r4_copies = []
    for b, (axis, m1, m2) in enumerate(ROUTES):
        other = "y" if axis == "x" else "x"
        low = min(m1, 2)
        r3_copies[b, 2].wait_recv()
        s_buf[b, 0, m2] = s_buf[b, 0, m2] + r3[b, 2 - low]
        r4_copies.append(send(s_buf.at[b, 0, m2], r4.at[b], to(other, m2)))
        r3_copies[b, m1].wait_recv()
        s_buf[b, 0, 0] = s_buf[b, 0, 0] + r3[b, m1 - low]

    z1_copies = []
    for b in (1, 2, 3):
        r4_copies[b].wait_recv()
        s_buf[b, 0, 0] = s_buf[b, 0, 0] + r4[b]
        z1_copies.append(send(s_buf.at[b, 0, 0], z1.at[b - 1], dev(dz=(0, 1, 2, -1)[b])))
    r4_copies[0].wait_recv()
    kept = s_buf[0, 0, 0].astype(F32) + r4[0].astype(F32)

    def project(jp):
        for jyh in range(2):
            for jx in range(4):
                owner = (yh + jyh - 2 * yh * jyh) * 8 + flip(x, jx) * 2
                half = par if jp == 0 else 1 - par
                lhs = jnp.concatenate(
                    [
                        normed[:, pl.ds(pl.multiple_of((owner + s) * 256 + half * 128, 128), 128)]
                        for s in range(2)
                    ],
                    axis=1,
                )
                part = jnp.dot(lhs, wg[jp, jyh, jx].reshape(256, 256), preferred_element_type=F32)
                if jp == 0 and jyh == 0 and jx == 0:
                    acc[...] = part
                else:
                    acc[...] += part

    for copy in z1_copies:
        copy.wait_recv()
    kept = kept + z1[0].astype(F32) + z1[1].astype(F32)
    late = z1[2].astype(F32)
    kept = kept + jnp.concatenate([late[7:8], late[0:7]], axis=0)
    zs[...] = kept.astype(BF16)
    pl.semaphore_wait(far_sem.at[2], 2)
    z2_copies = {a: send(zs.at[a], z2.at[a - 1], dev(dz=4 * a)) for a in (4, 3, 5, 2, 6, 1, 7)}

    nb.wait_recv()
    project(0)
    for copy in w5:
        copy.wait_recv()
    project(1)
    kx = send(acc.at[128:256], kr, dev(other=True))

    def rotate(source, half):
        for h in range(2):
            k = source[0:128, h * 128:(h + 1) * 128]
            turned = k * trig[0] + pltpu.roll(k, 64, 1) * trig[1]
            lanes = pl.ds(pl.multiple_of(half * 256 + h * 128, 128), 128)
            keys_ref[:, lanes] = turned.astype(BF16)

    rotate(acc, c)
    kx.wait_recv()
    rotate(kr, 1 - c)

    total = kept[0]
    for a in range(1, 8):
        z2_copies[a].wait_recv()
        total = total + z2[a - 1].astype(F32)
    grad_ref[...] = total

    for copy in sent:
        copy.wait_send()


def fused(x_this, grad_values, x_lower, gain, weight_lower, ids, freq):
    tiles = (8, 16, 128)
    anywhere = pl.BlockSpec(memory_space=pl.ANY)
    vmem = pl.BlockSpec(memory_space=pltpu.VMEM)
    return pl.pallas_call(
        kernel,
        out_shape=(
            jax.ShapeDtypeStruct((16, 128), F32),
            jax.ShapeDtypeStruct((128, 512), BF16),
        ),
        in_specs=[anywhere] * 7,
        out_specs=(vmem, vmem),
        scratch_shapes=[
            pltpu.VMEM((1, 128, 4096), BF16),
            pltpu.VMEM((1, 128, 512), BF16),
            pltpu.VMEM((1, 128, 4096), BF16),
            pltpu.VMEM((1, 4096), F32),
            pltpu.VMEM((256, 512), BF16),
            pltpu.VMEM((1, 128), jnp.int32),
            pltpu.VMEM((1, 128), F32),
            pltpu.VMEM((32, 2, 8, 128), F32),
            pltpu.VMEM((1024, 128), BF16),
            pltpu.VMEM((4, 2, 4, 2) + tiles, BF16),
            pltpu.VMEM((4, 2, 4, 2) + tiles, BF16),
            pltpu.VMEM((4, 4, 4) + tiles, BF16),
            pltpu.VMEM((4, 2, 4) + tiles, BF16),
            pltpu.VMEM((4, 4) + tiles, BF16),
            pltpu.VMEM((4, 2) + tiles, BF16),
            pltpu.VMEM((4,) + tiles, BF16),
            pltpu.VMEM((3,) + tiles, BF16),
            pltpu.VMEM((7, 16, 128), BF16),
            pltpu.VMEM(tiles, BF16),
            pltpu.VMEM((2, 2, 4, 2, 128, 256), BF16),
            pltpu.VMEM((256, 4096), BF16),
            pltpu.VMEM((256, 256), F32),
            pltpu.VMEM((128, 256), F32),
            pltpu.VMEM((4, 8, 128), F32),
            pltpu.VMEM((4, 8, 128), F32),
            pltpu.VMEM((2, 128, 128), F32),
            pltpu.SemaphoreType.DMA((7,)),
            pltpu.SemaphoreType.DMA((N_SEM,)),
            pltpu.SemaphoreType.DMA((N_SEM,)),
            pltpu.SemaphoreType.REGULAR((3,)),
        ],
        compiler_params=pltpu.CompilerParams(
            collective_id=0, has_side_effects=True, vmem_limit_bytes=60 * 1024 * 1024
        ),
        cost_estimate=pl.CostEstimate(
            flops=2 * 2 * 128 * 4096 * 512, bytes_accessed=4 * 1024 * 1024, transcendentals=32768
        ),
    )(x_this, grad_values, x_lower, gain, weight_lower, ids, freq)


def on_device(x_this, grad_values, x_lower, norm_gain, weight_lower, segment_ids):
    exponent = np.arange(128) % 64 * 2.0 / 128
    freq = jnp.asarray((500000.0 ** (-exponent)).astype(np.float32)[None])
    grad, keys = fused(
        x_this, grad_values, x_lower, norm_gain[None], weight_lower, segment_ids, freq
    )
    grad = grad.reshape(2, 8, 128).transpose(0, 2, 1).reshape(256, 8)
    return (grad, keys[None])


def solution(mesh):
    return jax.shard_map(
        on_device,
        mesh=mesh,
        in_specs=(
            P("dp", "node", None),
            P("dp", "node", None),
            P("dp", "node", None),
            P(),
            P("node", None),
            P("dp", "node"),
        ),
        out_specs=(P("node", "dp"), P("dp", "node", None)),
        check_vma=False,
    )
```

```python
import functools
import math

import jax
import jax.numpy as jnp
import numpy as np
from jax import lax
from jax.experimental import pallas as pl
from jax.experimental.pallas import tpu as pltpu
from jax.sharding import PartitionSpec as P

EPS = 1e-05
MESH = pl.DeviceIdType.MESH
F32 = jnp.float32
BF16 = jnp.bfloat16
N_SEM = 112
ORDER = (2, 1, 3, 0)
ROUTES = (("x", 1, 3), ("x", 3, 1), ("y", 1, 3), ("y", 3, 1))


def flip(v, mask):
    if mask == 0:
        return v
    if mask == 1:
        return v + 1 - 2 * lax.rem(v, 2)
    if mask == 2:
        return lax.rem(v + 2, 4)
    return 3 - v


def kernel(
    x_hbm, g_hbm, low_hbm, gain_hbm, w_hbm, ids_hbm, freq_hbm,
    grad_ref, keys_ref,
    x_v, g_v, low_v, gain_v, w_v, ids_v, freq_v,
    gt_f, gt2, c_send, c_recv, s_buf, r1, r2, r3, r4, z1, z2, zs,
    wg, normed, acc, kr, cs, cr, trig,
    local_sem, send_sem, recv_sem, far_sem,
):
    dp = lax.axis_index("dp")
    node = lax.axis_index("node")
    z, yl = lax.div(dp, 2), lax.rem(dp, 2)
    yh = lax.div(node, 8)
    x = lax.rem(lax.div(node, 2), 4)
    c = lax.rem(node, 2)
    y = yh * 2 + yl
    par = lax.rem(z, 2)

    def dev(jx=0, jy=0, dz=0, other=False):
        ty = flip(y, jy)
        tz = lax.rem(z + dz + 32, 32)
        tc = 1 - c if other else c
        return (tz * 2 + lax.rem(ty, 2), lax.div(ty, 2) * 8 + flip(x, jx) * 2 + tc)

    sent = []

    def send(src, dst, device):
        i = len(sent)
        copy = pltpu.make_async_remote_copy(
            src_ref=src, dst_ref=dst, send_sem=send_sem.at[i], recv_sem=recv_sem.at[i],
            device_id=device, device_id_type=MESH,
        )
        copy.start()
        sent.append(copy)
        return copy

    loads = []
    for src, dst in (
        (ids_hbm, ids_v), (g_hbm, g_v), (w_hbm, w_v), (x_hbm, x_v),
        (low_hbm, low_v), (gain_hbm, gain_v), (freq_hbm, freq_v),
    ):
        copy = pltpu.make_async_copy(src, dst, local_sem.at[len(loads)])
        copy.start()
        loads.append(copy)
    ld_ids, ld_g, ld_w, ld_x, ld_low, ld_gain, ld_freq = loads

    barrier = pltpu.get_barrier_semaphore()
    greet = [dev(other=True), dev(jx=1), dev(jx=3), dev(jy=1), dev(jy=3), dev(jy=2)]
    greet += [dev(dz=1), dev(dz=-1), dev(dz=2), dev(dz=-2)]
    for device in greet:
        pl.semaphore_signal(barrier, inc=1, device_id=device, device_id_type=MESH)

    ld_ids.wait()
    ids_row = jnp.broadcast_to(ids_v[...].astype(F32), (128, 128))
    sub = lax.broadcasted_iota(jnp.int32, (128, 128), 0)
    lane = lax.broadcasted_iota(jnp.int32, (128, 128), 1)
    id_col = jnp.sum(jnp.where(sub == lane, ids_row, 0.0), axis=1, keepdims=True)
    lane_f = lane.astype(F32)
    count = jnp.sum(jnp.where(id_col < lane_f, 1.0, 0.0), axis=0, keepdims=True)
    cs[0] = jnp.broadcast_to(count, (8, 128))

    ld_g.wait()
    gt_f[...] = g_v[0].astype(F32).T.reshape(32, 2, 8, 128)
    mine_first = jnp.concatenate([gt_f[:, yl], gt_f[:, 1 - yl]], axis=1).astype(BF16).reshape(512, 128)
    gt2[0:512, :] = mine_first
    gt2[512:1024, :] = mine_first
    g_rows = pl.ds(pl.multiple_of(z * 16, 16), 512)

    def term(jx, jyh, core):
        owner = (yh + jyh - 2 * yh * jyh) * 8 + flip(x, jx) * 2 + core
        lanes = pl.ds(pl.multiple_of(owner * 256, 256), 256)
        t = jnp.dot(gt2[g_rows, :], x_v[0, :, lanes], preferred_element_type=F32)
        t = t.reshape(8, 4, 2, 8, 256)

        def piece(b, jl):
            part = t[:, b, jl]
            return jnp.concatenate([part[:, :, :128], part[:, :, 128:]], axis=1)

        return piece

    def sibling_terms(jx):
        for jyh in (1, 0):
            piece = term(jx, jyh, 1 - c)
            for b in range(4):
                for jl in range(2):
                    c_send[jx, jyh, b, jl] = piece(b, jl).astype(BF16)

    ld_x.wait()
    sibling_terms(2)
    ld_w.wait()
    rows = pl.ds(pl.multiple_of(par * 128, 128), 128)
    away = pl.ds(pl.multiple_of((1 - c) * 256, 256), 256)
    here = pl.ds(pl.multiple_of(c * 256, 256), 256)
    wg[0, 0, 0, c] = w_v[rows, here]
    pl.semaphore_wait(barrier, len(greet))
    def far_signal(i):
        for side in (1, -1):
            pl.semaphore_signal(
                far_sem.at[i], inc=1, device_id=dev(dz=side * 2 * 2 ** i), device_id_type=MESH
            )

    far_signal(0)
    w0 = send(w_v.at[rows, away], wg.at[0, 0, 0, c], dev(other=True))
    cc = [send(cs.at[0], cr.at[0], dev(other=True))]
    w3, w4, w5 = {}, {}, []

    groups = (slice(0, 1), slice(1, 3), slice(3, 4))

    def spread_y(k):
        part = wg.at[0, 0, groups[k], 1 - yl]
        w3[k] = send(part, wg.at[0, 1, groups[k], 1 - yl], dev(jy=3))

    def spread_z(k):
        for core, dz in ((0, 1), (1, -1)):
            part = wg.at[0, 0, groups[k], core]
            w5.append(send(part, wg.at[1, 0, groups[k], core], dev(dz=dz)))

    def share(k):
        w3[k].wait_recv()
        part = wg.at[0, 1, groups[k], yl]
        w4[k] = send(part, wg.at[0, 1, groups[k], yl], dev(jy=1))
        w5.append(send(part, wg.at[1, 1, groups[k], yl], dev(dz=1 - 2 * yl)))

    def pass_on(k):
        w4[k].wait_recv()
        part = wg.at[0, 1, groups[k], 1 - yl]
        w5.append(send(part, wg.at[1, 1, groups[k], 1 - yl], dev(dz=2 * yl - 1)))

    c_copies = {}
    r1_copies = {}

    def for_sibling(jx):
        if jx != 2:
            sibling_terms(jx)
        for jyh in (1, 0):
            c_copies[jx, jyh] = send(c_send.at[jx, jyh], c_recv.at[jx, jyh], dev(other=True))

    def own(jx):
        for jyh in (1, 0):
            piece = term(jx, jyh, c)
            c_copies[jx, jyh].wait_recv()
            for b in range(4):
                for jl in range(2):
                    jy = jyh * 2 + jl
                    total = (piece(b, jl) + c_recv[jx, jyh, b, jl].astype(F32)).astype(BF16)
                    if b < 2:
                        s_buf[b, jx, jy] = total
                    else:
                        s_buf[b, jy, jx] = total
            pair = slice(jyh * 2, jyh * 2 + 2)
            for b, (axis, m1, m2) in enumerate(ROUTES):
                low = min(m1, 2)
                if axis == "x" and jx in (m1, 2):
                    r1_copies[b, jx, jyh] = send(
                        s_buf.at[b, jx, pair], r1.at[b, jx - low, pair], dev(jx=m1)
                    )
        for b, (axis, m1, m2) in enumerate(ROUTES):
            low = min(m1, 2)
            if axis == "y":
                r1_copies[b, jx] = send(
                    s_buf.at[b, low:low + 2, jx], r1.at[b, :, jx], dev(jy=m1)
                )

    for_sibling(2)
    for_sibling(1)
    own(2)
    w0.wait_recv()
    w1a = send(wg.at[0, 0, 0], wg.at[0, 0, 1], dev(jx=1))
    w1b = send(wg.at[0, 0, 0], wg.at[0, 0, 2], dev(jx=3))
    spread_y(0)
    spread_z(0)
    for_sibling(3)
    own(1)
    cc[0].wait_recv()
    cs[1] = cs[0] + cr[0]
    cc.append(send(cs.at[1], cr.at[1], dev(jx=1)))
    for_sibling(0)
    own(3)
    own(0)
    pl.semaphore_wait(far_sem.at[0], 2)
    far_signal(1)

    ld_low.wait()
    ld_gain.wait()
    gain = gain_v[...]

    def norm_rows(i, carry):
        rows = pl.ds(pl.multiple_of(i * 16, 16), 16)
        v = low_v[0, rows, :].astype(F32)
        mean_sq = jnp.sum(v * v, axis=1, keepdims=True) * (1.0 / 4096)
        normed[rows, :] = (v * lax.rsqrt(mean_sq + EPS) * gain).astype(BF16)
        return carry

    lax.fori_loop(0, 2, norm_rows, 0)

    def to(axis, mask):
        return dev(jx=mask) if axis == "x" else dev(jy=mask)

    r2_copies = {}
    for jx in ORDER:
        for b, (axis, m1, m2) in enumerate(ROUTES):
            low = min(m1, 2)
            if axis == "x":
                if jx not in (m1, 2):
                    continue
                slot = m2 if jx == 2 else 0
                for jyh in (1, 0):
                    pair = slice(jyh * 2, jyh * 2 + 2)
                    r1_copies[b, jx, jyh].wait_recv()
                    s_buf[b, slot, pair] = s_buf[b, slot, pair] + r1[b, jx - low, pair]
                    if slot:
                        r2_copies[b, jyh] = send(
                            s_buf.at[b, m2, pair], r2.at[b, pair], to(axis, m2)
                        )
            else:
                r1_copies[b, jx].wait_recv()
                s_buf[b, m2, jx] = s_buf[b, m2, jx] + r1[b, 2 - low, jx]
                r2_copies[b, jx] = send(s_buf.at[b, m2, jx], r2.at[b, jx], to(axis, m2))
                s_buf[b, 0, jx] = s_buf[b, 0, jx] + r1[b, m1 - low, jx]

    cc[1].wait_recv()
    cs[2] = cs[1] + cr[1]
    cc.append(send(cs.at[2], cr.at[2], dev(jx=3)))
    w1a.wait_recv()
    w1b.wait_recv()
    w2a = send(wg.at[0, 0, 2, 0], wg.at[0, 0, 3, 0], dev(jx=1))
    w2b = send(wg.at[0, 0, 1, 1], wg.at[0, 0, 3, 1], dev(jx=3))
    spread_y(1)
    spread_z(1)
    share(0)
    lax.fori_loop(2, 5, norm_rows, 0)

    r3_copies = {}

    def forward(b, s, other, m1):
        s_buf[b, 0, s] = s_buf[b, 0, s] + r2[b, s]
        if s in (m1, 2):
            r3_copies[b, s] = send(s_buf.at[b, 0, s], r3.at[b, s - min(m1, 2)], to(other, m1))

    for jx in ORDER:
        for b, (axis, m1, m2) in enumerate(ROUTES):
            if axis == "y":
                r2_copies[b, jx].wait_recv()
                forward(b, jx, "x", m1)
            elif jx in (2, 1):
                jyh = jx - 1
                r2_copies[b, jyh].wait_recv()
                for s in (2, 3) if jyh else (1, 0):
                    forward(b, s, "y", m1)

    cc[2].wait_recv()
    cs[3] = cs[2] + cr[2]
    cc.append(send(cs.at[3], cr.at[3], dev(jy=2)))
    pl.semaphore_wait(far_sem.at[1], 2)
    far_signal(2)
    lax.fori_loop(5, 8, norm_rows, 0)
    nb = send(normed.at[0:128], normed.at[128:256], dev(other=True))

    pass_on(0)

    r4_copies = []
    for b, (axis, m1, m2) in enumerate(ROUTES):
        other = "y" if axis == "x" else "x"
        low = min(m1, 2)
        r3_copies[b, 2].wait_recv()
        s_buf[b, 0, m2] = s_buf[b, 0, m2] + r3[b, 2 - low]
        r4_copies.append(send(s_buf.at[b, 0, m2], r4.at[b], to(other, m2)))
        r3_copies[b, m1].wait_recv()
        s_buf[b, 0, 0] = s_buf[b, 0, 0] + r3[b, m1 - low]

    w2a.wait_recv()
    w2b.wait_recv()
    spread_y(2)
    spread_z(2)

    z1_copies = []
    for b in (1, 2, 3):
        r4_copies[b].wait_recv()
        s_buf[b, 0, 0] = s_buf[b, 0, 0] + r4[b]
        z1_copies.append(send(s_buf.at[b, 0, 0], z1.at[b - 1], dev(dz=(0, 1, 2, -1)[b])))
    r4_copies[0].wait_recv()
    kept = s_buf[0, 0, 0].astype(F32) + r4[0].astype(F32)
    share(1)

    cc[3].wait_recv()
    counts = (cs[3] + cr[3])[0:1]
    start = jnp.sum(jnp.where(lane_f == id_col, counts, 0.0), axis=1, keepdims=True)
    first_token = (node * 128).astype(F32)
    token = lax.broadcasted_iota(jnp.int32, (128, 1), 0).astype(F32)
    positions = token + first_token - start
    ld_freq.wait()
    angle = positions * freq_v[...]
    trig[0] = jnp.cos(angle)
    trig[1] = jnp.where(lane < 64, -1.0, 1.0) * jnp.sin(angle)


    def project(jp, jyh):
        for slot, jx in enumerate((0, 1, 3, 2)):
            owner = (yh + jyh - 2 * yh * jyh) * 8 + flip(x, jx) * 2
            half = par if jp == 0 else 1 - par
            lhs = jnp.concatenate(
                [
                    normed[:, pl.ds(pl.multiple_of((owner + s) * 256 + half * 128, 128), 128)]
                    for s in range(2)
                ],
                axis=1,
            )
            part = jnp.dot(lhs, wg[jp, jyh, slot].reshape(256, 256), preferred_element_type=F32)
            if jp == 0 and jyh == 0 and jx == 0:
                acc[...] = part
            else:
                acc[...] += part

    for copy in z1_copies:
        copy.wait_recv()
    kept = kept + z1[0].astype(F32) + z1[1].astype(F32)
    late = z1[2].astype(F32)
    kept = kept + jnp.concatenate([late[7:8], late[0:7]], axis=0)
    zs[...] = kept.astype(BF16)
    pl.semaphore_wait(far_sem.at[2], 2)
    z2_copies = {a: send(zs.at[a], z2.at[a - 1], dev(dz=4 * a)) for a in (4, 3, 5, 2, 6, 1, 7)}

    share(2)
    pass_on(1)
    nb.wait_recv()
    project(0, 0)
    pass_on(2)
    project(0, 1)
    for copy in w5:
        copy.wait_recv()
    project(1, 0)
    project(1, 1)
    kx = send(acc.at[128:256], kr, dev(other=True))

    def rotate(source, half):
        for h in range(2):
            k = source[0:128, h * 128:(h + 1) * 128]
            turned = k * trig[0] + pltpu.roll(k, 64, 1) * trig[1]
            lanes = pl.ds(pl.multiple_of(half * 256 + h * 128, 128), 128)
            keys_ref[:, lanes] = turned.astype(BF16)

    rotate(acc, c)
    kx.wait_recv()
    rotate(kr, 1 - c)

    total = kept[0]
    for a in range(1, 8):
        z2_copies[a].wait_recv()
        total = total + z2[a - 1].astype(F32)
    grad_ref[...] = total

    for copy in sent:
        copy.wait_send()


def fused(x_this, grad_values, x_lower, gain, weight_lower, ids, freq):
    tiles = (8, 16, 128)
    anywhere = pl.BlockSpec(memory_space=pl.ANY)
    vmem = pl.BlockSpec(memory_space=pltpu.VMEM)
    return pl.pallas_call(
        kernel,
        out_shape=(
            pltpu.VMEM((16, 128), F32),
            pltpu.VMEM((128, 512), BF16),
        ),
        in_specs=[anywhere] * 7,
        out_specs=(vmem, vmem),
        scratch_shapes=[
            pltpu.VMEM((1, 128, 4096), BF16),
            pltpu.VMEM((1, 128, 512), BF16),
            pltpu.VMEM((1, 128, 4096), BF16),
            pltpu.VMEM((1, 4096), F32),
            pltpu.VMEM((256, 512), BF16),
            pltpu.VMEM((1, 128), jnp.int32),
            pltpu.VMEM((1, 128), F32),
            pltpu.VMEM((32, 2, 8, 128), F32),
            pltpu.VMEM((1024, 128), BF16),
            pltpu.VMEM((4, 2, 4, 2) + tiles, BF16),
            pltpu.VMEM((4, 2, 4, 2) + tiles, BF16),
            pltpu.VMEM((4, 4, 4) + tiles, BF16),
            pltpu.VMEM((4, 2, 4) + tiles, BF16),
            pltpu.VMEM((4, 4) + tiles, BF16),
            pltpu.VMEM((4, 2) + tiles, BF16),
            pltpu.VMEM((4,) + tiles, BF16),
            pltpu.VMEM((3,) + tiles, BF16),
            pltpu.VMEM((7, 16, 128), BF16),
            pltpu.VMEM(tiles, BF16),
            pltpu.VMEM((2, 2, 4, 2, 128, 256), BF16),
            pltpu.VMEM((256, 4096), BF16),
            pltpu.VMEM((256, 256), F32),
            pltpu.VMEM((128, 256), F32),
            pltpu.VMEM((4, 8, 128), F32),
            pltpu.VMEM((4, 8, 128), F32),
            pltpu.VMEM((2, 128, 128), F32),
            pltpu.SemaphoreType.DMA((7,)),
            pltpu.SemaphoreType.DMA((N_SEM,)),
            pltpu.SemaphoreType.DMA((N_SEM,)),
            pltpu.SemaphoreType.REGULAR((3,)),
        ],
        compiler_params=pltpu.CompilerParams(
            collective_id=0, has_side_effects=True, vmem_limit_bytes=60 * 1024 * 1024
        ),
        cost_estimate=pl.CostEstimate(
            flops=2 * 2 * 128 * 4096 * 512, bytes_accessed=4 * 1024 * 1024, transcendentals=32768
        ),
    )(x_this, grad_values, x_lower, gain, weight_lower, ids, freq)


def on_device(x_this, grad_values, x_lower, norm_gain, weight_lower, segment_ids):
    exponent = np.arange(128) % 64 * 2.0 / 128
    freq = jnp.asarray((500000.0 ** (-exponent)).astype(np.float32)[None])
    grad, keys = fused(
        x_this, grad_values, x_lower, norm_gain[None], weight_lower, segment_ids, freq
    )
    grad = grad.reshape(2, 8, 128).transpose(0, 2, 1).reshape(256, 8)
    return (grad, keys[None])


def solution(mesh):
    return jax.shard_map(
        on_device,
        mesh=mesh,
        in_specs=(
            P("dp", "node", None),
            P("dp", "node", None),
            P("dp", "node", None),
            P(),
            P("node", None),
            P("dp", "node"),
        ),
        out_specs=(P("node", "dp"), P("dp", "node", None)),
        check_vma=False,
    )
```

```python
import functools
import math

import jax
import jax.numpy as jnp
import numpy as np
from jax import lax
from jax.experimental import pallas as pl
from jax.experimental.pallas import tpu as pltpu
from jax.sharding import PartitionSpec as P

EPS = 1e-05
MESH = pl.DeviceIdType.MESH
F32 = jnp.float32
BF16 = jnp.bfloat16
N_SEM = 112
ORDER = (2, 1, 3, 0)
ROUTES = (("x", 1, 3), ("x", 3, 1), ("y", 1, 3), ("y", 3, 1))


def flip(v, mask):
    if mask == 0:
        return v
    if mask == 1:
        return v + 1 - 2 * lax.rem(v, 2)
    if mask == 2:
        return lax.rem(v + 2, 4)
    return 3 - v


def kernel(
    x_hbm, g_hbm, low_hbm, gain_hbm, w_hbm, ids_hbm, freq_hbm,
    grad_ref, keys_ref,
    x_v, g_v, low_v, gain_v, w_v, ids_v, freq_v,
    gt_f, gt2, c_send, c_recv, s_buf, r1, r2, r3, r4, z1, z2, zs,
    wg, normed, acc, kr, cs, cr, trig,
    local_sem, send_sem, recv_sem, far_sem,
):
    dp = lax.axis_index("dp")
    node = lax.axis_index("node")
    z, yl = lax.div(dp, 2), lax.rem(dp, 2)
    yh = lax.div(node, 8)
    x = lax.rem(lax.div(node, 2), 4)
    c = lax.rem(node, 2)
    y = yh * 2 + yl
    par = lax.rem(z, 2)

    def dev(jx=0, jy=0, dz=0, other=False):
        ty = flip(y, jy)
        tz = lax.rem(z + dz + 32, 32)
        tc = 1 - c if other else c
        return (tz * 2 + lax.rem(ty, 2), lax.div(ty, 2) * 8 + flip(x, jx) * 2 + tc)

    sent = []

    def send(src, dst, device):
        i = len(sent)
        copy = pltpu.make_async_remote_copy(
            src_ref=src, dst_ref=dst, send_sem=send_sem.at[i], recv_sem=recv_sem.at[i],
            device_id=device, device_id_type=MESH,
        )
        copy.start()
        sent.append(copy)
        return copy

    loads = []
    for src, dst in (
        (ids_hbm, ids_v), (g_hbm, g_v), (w_hbm, w_v), (x_hbm, x_v),
        (low_hbm, low_v), (gain_hbm, gain_v), (freq_hbm, freq_v),
    ):
        copy = pltpu.make_async_copy(src, dst, local_sem.at[len(loads)])
        copy.start()
        loads.append(copy)
    ld_ids, ld_g, ld_w, ld_x, ld_low, ld_gain, ld_freq = loads

    barrier = pltpu.get_barrier_semaphore()
    greet = [dev(other=True), dev(jx=1), dev(jx=3), dev(jy=1), dev(jy=3), dev(jy=2)]
    greet += [dev(dz=1), dev(dz=-1), dev(dz=2), dev(dz=-2)]
    for device in greet:
        pl.semaphore_signal(barrier, inc=1, device_id=device, device_id_type=MESH)

    ld_ids.wait()
    ids_row = jnp.broadcast_to(ids_v[...].astype(F32), (128, 128))
    sub = lax.broadcasted_iota(jnp.int32, (128, 128), 0)
    lane = lax.broadcasted_iota(jnp.int32, (128, 128), 1)
    id_col = jnp.sum(jnp.where(sub == lane, ids_row, 0.0), axis=1, keepdims=True)
    lane_f = lane.astype(F32)
    count = jnp.sum(jnp.where(id_col < lane_f, 1.0, 0.0), axis=0, keepdims=True)
    cs[0] = jnp.broadcast_to(count, (8, 128))

    ld_g.wait()
    gt_f[...] = g_v[0].astype(F32).T.reshape(32, 2, 8, 128)
    mine_first = jnp.concatenate([gt_f[:, yl], gt_f[:, 1 - yl]], axis=1).astype(BF16).reshape(512, 128)
    gt2[0:512, :] = mine_first
    gt2[512:1024, :] = mine_first
    g_rows = pl.ds(pl.multiple_of(z * 16, 16), 512)

    def term(jx, jyh, core):
        owner = (yh + jyh - 2 * yh * jyh) * 8 + flip(x, jx) * 2 + core
        lanes = pl.ds(pl.multiple_of(owner * 256, 256), 256)
        t = jnp.dot(gt2[g_rows, :], x_v[0, :, lanes], preferred_element_type=F32)
        t = t.reshape(8, 4, 2, 8, 256)

        def piece(b, jl):
            part = t[:, b, jl]
            return jnp.concatenate([part[:, :, :128], part[:, :, 128:]], axis=1)

        return piece

    def sibling_terms(jx):
        for jyh in (1, 0):
            piece = term(jx, jyh, 1 - c)
            for b in range(4):
                for jl in range(2):
                    c_send[jx, jyh, b, jl] = piece(b, jl).astype(BF16)

    ld_x.wait()
    sibling_terms(2)
    ld_w.wait()
    rows = pl.ds(pl.multiple_of(par * 128, 128), 128)
    away = pl.ds(pl.multiple_of((1 - c) * 256, 256), 256)
    here = pl.ds(pl.multiple_of(c * 256, 256), 256)
    wg[0, 0, 0, c] = w_v[rows, here]
    pl.semaphore_wait(barrier, len(greet))
    def far_signal(i):
        for side in (1, -1):
            pl.semaphore_signal(
                far_sem.at[i], inc=1, device_id=dev(dz=side * 2 * 2 ** i), device_id_type=MESH
            )

    far_signal(0)
    w0 = send(w_v.at[rows, away], wg.at[0, 0, 0, c], dev(other=True))
    cc = [send(cs.at[0], cr.at[0], dev(other=True))]
    w3, w4, w5 = {}, {}, ([], [])

    groups = (slice(0, 1), slice(1, 3), slice(3, 4))

    def spread_y(k):
        part = wg.at[0, 0, groups[k], 1 - yl]
        w3[k] = send(part, wg.at[0, 1, groups[k], 1 - yl], dev(jy=3))

    def spread_z(k):
        for core, dz in ((0, 1), (1, -1)):
            part = wg.at[0, 0, groups[k], core]
            w5[0].append(send(part, wg.at[1, 0, groups[k], core], dev(dz=dz)))

    def share(k):
        w3[k].wait_recv()
        part = wg.at[0, 1, groups[k], yl]
        w4[k] = send(part, wg.at[0, 1, groups[k], yl], dev(jy=1))
        w5[1].append(send(part, wg.at[1, 1, groups[k], yl], dev(dz=1 - 2 * yl)))

    def pass_on(k):
        w4[k].wait_recv()
        part = wg.at[0, 1, groups[k], 1 - yl]
        w5[1].append(send(part, wg.at[1, 1, groups[k], 1 - yl], dev(dz=2 * yl - 1)))

    c_copies = {}
    r1_copies = {}

    def for_sibling(jx):
        if jx != 2:
            sibling_terms(jx)
        for jyh in (1, 0):
            c_copies[jx, jyh] = send(c_send.at[jx, jyh], c_recv.at[jx, jyh], dev(other=True))

    def own(jx):
        for jyh in (1, 0):
            piece = term(jx, jyh, c)
            c_copies[jx, jyh].wait_recv()
            for b in range(4):
                for jl in range(2):
                    jy = jyh * 2 + jl
                    total = (piece(b, jl) + c_recv[jx, jyh, b, jl].astype(F32)).astype(BF16)
                    if b < 2:
                        s_buf[b, jx, jy] = total
                    else:
                        s_buf[b, jy, jx] = total
            pair = slice(jyh * 2, jyh * 2 + 2)
            for b, (axis, m1, m2) in enumerate(ROUTES):
                low = min(m1, 2)
                if axis == "x" and jx in (m1, 2):
                    r1_copies[b, jx, jyh] = send(
                        s_buf.at[b, jx, pair], r1.at[b, jx - low, pair], dev(jx=m1)
                    )
        for b, (axis, m1, m2) in enumerate(ROUTES):
            low = min(m1, 2)
            if axis == "y":
                r1_copies[b, jx] = send(
                    s_buf.at[b, low:low + 2, jx], r1.at[b, :, jx], dev(jy=m1)
                )

    for_sibling(2)
    for_sibling(1)
    own(2)
    for_sibling(3)
    own(1)
    cc[0].wait_recv()
    cs[1] = cs[0] + cr[0]
    cc.append(send(cs.at[1], cr.at[1], dev(jx=1)))
    for_sibling(0)
    own(3)
    own(0)
    w0.wait_recv()
    w1a = send(wg.at[0, 0, 0], wg.at[0, 0, 1], dev(jx=1))
    w1b = send(wg.at[0, 0, 0], wg.at[0, 0, 2], dev(jx=3))
    spread_y(0)
    spread_z(0)
    pl.semaphore_wait(far_sem.at[0], 2)
    far_signal(1)

    ld_low.wait()
    ld_gain.wait()
    gain = gain_v[...]

    def norm_rows(i, carry):
        rows = pl.ds(pl.multiple_of(i * 16, 16), 16)
        v = low_v[0, rows, :].astype(F32)
        mean_sq = jnp.sum(v * v, axis=1, keepdims=True) * (1.0 / 4096)
        normed[rows, :] = (v * lax.rsqrt(mean_sq + EPS) * gain).astype(BF16)
        return carry

    lax.fori_loop(0, 2, norm_rows, 0)

    def to(axis, mask):
        return dev(jx=mask) if axis == "x" else dev(jy=mask)

    r2_copies = {}
    for jx in ORDER:
        for b, (axis, m1, m2) in enumerate(ROUTES):
            low = min(m1, 2)
            if axis == "x":
                if jx not in (m1, 2):
                    continue
                slot = m2 if jx == 2 else 0
                for jyh in (1, 0):
                    pair = slice(jyh * 2, jyh * 2 + 2)
                    r1_copies[b, jx, jyh].wait_recv()
                    s_buf[b, slot, pair] = s_buf[b, slot, pair] + r1[b, jx - low, pair]
                    if slot:
                        r2_copies[b, jyh] = send(
                            s_buf.at[b, m2, pair], r2.at[b, pair], to(axis, m2)
                        )
            else:
                r1_copies[b, jx].wait_recv()
                s_buf[b, m2, jx] = s_buf[b, m2, jx] + r1[b, 2 - low, jx]
                r2_copies[b, jx] = send(s_buf.at[b, m2, jx], r2.at[b, jx], to(axis, m2))
                s_buf[b, 0, jx] = s_buf[b, 0, jx] + r1[b, m1 - low, jx]

    cc[1].wait_recv()
    cs[2] = cs[1] + cr[1]
    cc.append(send(cs.at[2], cr.at[2], dev(jx=3)))
    lax.fori_loop(2, 5, norm_rows, 0)

    r3_copies = {}

    def forward(b, s, other, m1):
        s_buf[b, 0, s] = s_buf[b, 0, s] + r2[b, s]
        if s in (m1, 2):
            r3_copies[b, s] = send(s_buf.at[b, 0, s], r3.at[b, s - min(m1, 2)], to(other, m1))

    for jx in ORDER:
        for b, (axis, m1, m2) in enumerate(ROUTES):
            if axis == "y":
                r2_copies[b, jx].wait_recv()
                forward(b, jx, "x", m1)
            elif jx in (2, 1):
                jyh = jx - 1
                r2_copies[b, jyh].wait_recv()
                for s in (2, 3) if jyh else (1, 0):
                    forward(b, s, "y", m1)

    cc[2].wait_recv()
    cs[3] = cs[2] + cr[2]
    cc.append(send(cs.at[3], cr.at[3], dev(jy=2)))
    pl.semaphore_wait(far_sem.at[1], 2)
    far_signal(2)
    lax.fori_loop(5, 8, norm_rows, 0)
    nb = send(normed.at[0:128], normed.at[128:256], dev(other=True))


    w1a.wait_recv()
    w1b.wait_recv()
    w2a = send(wg.at[0, 0, 2, 0], wg.at[0, 0, 3, 0], dev(jx=1))
    w2b = send(wg.at[0, 0, 1, 1], wg.at[0, 0, 3, 1], dev(jx=3))
    spread_y(1)
    spread_z(1)
    share(0)

    r4_copies = []
    for b, (axis, m1, m2) in enumerate(ROUTES):
        other = "y" if axis == "x" else "x"
        low = min(m1, 2)
        r3_copies[b, 2].wait_recv()
        s_buf[b, 0, m2] = s_buf[b, 0, m2] + r3[b, 2 - low]
        r4_copies.append(send(s_buf.at[b, 0, m2], r4.at[b], to(other, m2)))
        r3_copies[b, m1].wait_recv()
        s_buf[b, 0, 0] = s_buf[b, 0, 0] + r3[b, m1 - low]

    z1_copies = []
    for b in (1, 2, 3):
        r4_copies[b].wait_recv()
        s_buf[b, 0, 0] = s_buf[b, 0, 0] + r4[b]
        z1_copies.append(send(s_buf.at[b, 0, 0], z1.at[b - 1], dev(dz=(0, 1, 2, -1)[b])))
    r4_copies[0].wait_recv()
    kept = s_buf[0, 0, 0].astype(F32) + r4[0].astype(F32)
    pass_on(0)

    cc[3].wait_recv()
    counts = (cs[3] + cr[3])[0:1]
    start = jnp.sum(jnp.where(lane_f == id_col, counts, 0.0), axis=1, keepdims=True)
    first_token = (node * 128).astype(F32)
    token = lax.broadcasted_iota(jnp.int32, (128, 1), 0).astype(F32)
    positions = token + first_token - start
    ld_freq.wait()
    angle = positions * freq_v[...]
    trig[0] = jnp.cos(angle)
    trig[1] = jnp.where(lane < 64, -1.0, 1.0) * jnp.sin(angle)


    def project(jp, jyh):
        for slot, jx in enumerate((0, 1, 3, 2)):
            owner = (yh + jyh - 2 * yh * jyh) * 8 + flip(x, jx) * 2
            half = par if jp == 0 else 1 - par
            lhs = jnp.concatenate(
                [
                    normed[:, pl.ds(pl.multiple_of((owner + s) * 256 + half * 128, 128), 128)]
                    for s in range(2)
                ],
                axis=1,
            )
            part = jnp.dot(lhs, wg[jp, jyh, slot].reshape(256, 256), preferred_element_type=F32)
            if jp == 0 and jyh == 0 and jx == 0:
                acc[...] = part
            else:
                acc[...] += part

    w2a.wait_recv()
    w2b.wait_recv()
    spread_y(2)
    spread_z(2)
    share(1)
    nb.wait_recv()
    project(0, 0)

    for copy in z1_copies:
        copy.wait_recv()
    kept = kept + z1[0].astype(F32) + z1[1].astype(F32)
    late = z1[2].astype(F32)
    kept = kept + jnp.concatenate([late[7:8], late[0:7]], axis=0)
    zs[...] = kept.astype(BF16)
    pl.semaphore_wait(far_sem.at[2], 2)
    z2_copies = {a: send(zs.at[a], z2.at[a - 1], dev(dz=4 * a)) for a in (4, 3, 5, 2, 6, 1, 7)}

    share(2)
    pass_on(1)
    pass_on(2)
    project(0, 1)
    for jyh in range(2):
        for copy in w5[jyh]:
            copy.wait_recv()
        project(1, jyh)
    kx = send(acc.at[128:256], kr, dev(other=True))

    def rotate(source, half):
        for h in range(2):
            k = source[0:128, h * 128:(h + 1) * 128]
            turned = k * trig[0] + pltpu.roll(k, 64, 1) * trig[1]
            lanes = pl.ds(pl.multiple_of(half * 256 + h * 128, 128), 128)
            keys_ref[:, lanes] = turned.astype(BF16)

    rotate(acc, c)
    kx.wait_recv()
    rotate(kr, 1 - c)

    total = kept[0]
    for a in range(1, 8):
        z2_copies[a].wait_recv()
        total = total + z2[a - 1].astype(F32)
    grad_ref[...] = total

    for copy in sent:
        copy.wait_send()


def fused(x_this, grad_values, x_lower, gain, weight_lower, ids, freq):
    tiles = (8, 16, 128)
    anywhere = pl.BlockSpec(memory_space=pl.ANY)
    vmem = pl.BlockSpec(memory_space=pltpu.VMEM)
    return pl.pallas_call(
        kernel,
        out_shape=(
            pltpu.VMEM((16, 128), F32),
            pltpu.VMEM((128, 512), BF16),
        ),
        in_specs=[anywhere] * 7,
        out_specs=(vmem, vmem),
        scratch_shapes=[
            pltpu.VMEM((1, 128, 4096), BF16),
            pltpu.VMEM((1, 128, 512), BF16),
            pltpu.VMEM((1, 128, 4096), BF16),
            pltpu.VMEM((1, 4096), F32),
            pltpu.VMEM((256, 512), BF16),
            pltpu.VMEM((1, 128), jnp.int32),
            pltpu.VMEM((1, 128), F32),
            pltpu.VMEM((32, 2, 8, 128), F32),
            pltpu.VMEM((1024, 128), BF16),
            pltpu.VMEM((4, 2, 4, 2) + tiles, BF16),
            pltpu.VMEM((4, 2, 4, 2) + tiles, BF16),
            pltpu.VMEM((4, 4, 4) + tiles, BF16),
            pltpu.VMEM((4, 2, 4) + tiles, BF16),
            pltpu.VMEM((4, 4) + tiles, BF16),
            pltpu.VMEM((4, 2) + tiles, BF16),
            pltpu.VMEM((4,) + tiles, BF16),
            pltpu.VMEM((3,) + tiles, BF16),
            pltpu.VMEM((7, 16, 128), BF16),
            pltpu.VMEM(tiles, BF16),
            pltpu.VMEM((2, 2, 4, 2, 128, 256), BF16),
            pltpu.VMEM((256, 4096), BF16),
            pltpu.VMEM((256, 256), F32),
            pltpu.VMEM((128, 256), F32),
            pltpu.VMEM((4, 8, 128), F32),
            pltpu.VMEM((4, 8, 128), F32),
            pltpu.VMEM((2, 128, 128), F32),
            pltpu.SemaphoreType.DMA((7,)),
            pltpu.SemaphoreType.DMA((N_SEM,)),
            pltpu.SemaphoreType.DMA((N_SEM,)),
            pltpu.SemaphoreType.REGULAR((3,)),
        ],
        compiler_params=pltpu.CompilerParams(
            collective_id=0, has_side_effects=True, vmem_limit_bytes=60 * 1024 * 1024
        ),
        cost_estimate=pl.CostEstimate(
            flops=2 * 2 * 128 * 4096 * 512, bytes_accessed=4 * 1024 * 1024, transcendentals=32768
        ),
    )(x_this, grad_values, x_lower, gain, weight_lower, ids, freq)


def on_device(x_this, grad_values, x_lower, norm_gain, weight_lower, segment_ids):
    exponent = np.arange(128) % 64 * 2.0 / 128
    freq = jnp.asarray((500000.0 ** (-exponent)).astype(np.float32)[None])
    grad, keys = fused(
        x_this, grad_values, x_lower, norm_gain[None], weight_lower, segment_ids, freq
    )
    grad = grad.reshape(2, 8, 128).transpose(0, 2, 1).reshape(256, 8)
    return (grad, keys[None])


def solution(mesh):
    return jax.shard_map(
        on_device,
        mesh=mesh,
        in_specs=(
            P("dp", "node", None),
            P("dp", "node", None),
            P("dp", "node", None),
            P(),
            P("node", None),
            P("dp", "node"),
        ),
        out_specs=(P("node", "dp"), P("dp", "node", None)),
        check_vma=False,
    )
```

```python
import functools
import math

import jax
import jax.numpy as jnp
import numpy as np
from jax import lax
from jax.experimental import pallas as pl
from jax.experimental.pallas import tpu as pltpu
from jax.sharding import PartitionSpec as P

EPS = 1e-05
MESH = pl.DeviceIdType.MESH
F32 = jnp.float32
BF16 = jnp.bfloat16
N_SEM = 112
ORDER = (2, 1, 3, 0)
ROUTES = (("x", 1, 3), ("x", 3, 1), ("y", 1, 3), ("y", 3, 1))


def flip(v, mask):
    if mask == 0:
        return v
    if mask == 1:
        return v + 1 - 2 * lax.rem(v, 2)
    if mask == 2:
        return lax.rem(v + 2, 4)
    return 3 - v


def kernel(
    x_hbm, g_hbm, low_hbm, gain_hbm, w_hbm, ids_hbm, freq_hbm,
    grad_ref, keys_ref,
    x_v, g_v, low_v, gain_v, w_v, ids_v, freq_v,
    gt_f, gt2, c_send, c_recv, s_buf, r1, r2, r3, r4, z1, z2, zs,
    wg, normed, acc, kr, cs, cr, trig,
    local_sem, send_sem, recv_sem, far_sem,
):
    dp = lax.axis_index("dp")
    node = lax.axis_index("node")
    z, yl = lax.div(dp, 2), lax.rem(dp, 2)
    yh = lax.div(node, 8)
    x = lax.rem(lax.div(node, 2), 4)
    c = lax.rem(node, 2)
    y = yh * 2 + yl
    par = lax.rem(z, 2)

    def dev(jx=0, jy=0, dz=0, other=False):
        ty = flip(y, jy)
        tz = lax.rem(z + dz + 32, 32)
        tc = 1 - c if other else c
        return (tz * 2 + lax.rem(ty, 2), lax.div(ty, 2) * 8 + flip(x, jx) * 2 + tc)

    sent = []

    def send(src, dst, device):
        i = len(sent)
        copy = pltpu.make_async_remote_copy(
            src_ref=src, dst_ref=dst, send_sem=send_sem.at[i], recv_sem=recv_sem.at[i],
            device_id=device, device_id_type=MESH,
        )
        copy.start()
        sent.append(copy)
        return copy

    loads = []
    for src, dst in (
        (ids_hbm, ids_v), (g_hbm, g_v), (w_hbm, w_v), (x_hbm, x_v),
        (low_hbm, low_v), (gain_hbm, gain_v), (freq_hbm, freq_v),
    ):
        copy = pltpu.make_async_copy(src, dst, local_sem.at[len(loads)])
        copy.start()
        loads.append(copy)
    ld_ids, ld_g, ld_w, ld_x, ld_low, ld_gain, ld_freq = loads

    barrier = pltpu.get_barrier_semaphore()
    greet = [dev(other=True), dev(jx=1), dev(jx=3), dev(jy=1), dev(jy=3), dev(jy=2)]
    greet += [dev(dz=1), dev(dz=-1), dev(dz=2), dev(dz=-2)]
    for device in greet:
        pl.semaphore_signal(barrier, inc=1, device_id=device, device_id_type=MESH)

    ld_ids.wait()
    ids_row = jnp.broadcast_to(ids_v[...].astype(F32), (128, 128))
    sub = lax.broadcasted_iota(jnp.int32, (128, 128), 0)
    lane = lax.broadcasted_iota(jnp.int32, (128, 128), 1)
    id_col = jnp.sum(jnp.where(sub == lane, ids_row, 0.0), axis=1, keepdims=True)
    lane_f = lane.astype(F32)
    count = jnp.sum(jnp.where(id_col < lane_f, 1.0, 0.0), axis=0, keepdims=True)
    cs[0] = jnp.broadcast_to(count, (8, 128))

    ld_g.wait()
    gt_f[...] = g_v[0].astype(F32).T.reshape(32, 2, 8, 128)
    mine_first = jnp.concatenate([gt_f[:, yl], gt_f[:, 1 - yl]], axis=1).astype(BF16).reshape(512, 128)
    gt2[0:512, :] = mine_first
    gt2[512:1024, :] = mine_first
    g_rows = pl.ds(pl.multiple_of(z * 16, 16), 512)

    def term(jx, jyh, core):
        owner = (yh + jyh - 2 * yh * jyh) * 8 + flip(x, jx) * 2 + core
        lanes = pl.ds(pl.multiple_of(owner * 256, 256), 256)
        t = jnp.dot(gt2[g_rows, :], x_v[0, :, lanes], preferred_element_type=F32)
        t = t.reshape(8, 4, 2, 8, 256)

        def piece(b, jl):
            part = t[:, b, jl]
            return jnp.concatenate([part[:, :, :128], part[:, :, 128:]], axis=1)

        return piece

    def sibling_terms(jx):
        for jyh in (1, 0):
            piece = term(jx, jyh, 1 - c)
            for b in range(4):
                for jl in range(2):
                    c_send[jx, jyh, b, jl] = piece(b, jl).astype(BF16)

    ld_x.wait()
    sibling_terms(2)
    ld_w.wait()
    rows = pl.ds(pl.multiple_of(par * 128, 128), 128)
    away = pl.ds(pl.multiple_of((1 - c) * 256, 256), 256)
    here = pl.ds(pl.multiple_of(c * 256, 256), 256)
    wg[0, 0, 0, c] = w_v[rows, here]
    pl.semaphore_wait(barrier, len(greet))
    def far_signal(i):
        for side in (1, -1):
            pl.semaphore_signal(
                far_sem.at[i], inc=1, device_id=dev(dz=side * 2 * 2 ** i), device_id_type=MESH
            )

    far_signal(0)
    w0 = send(w_v.at[rows, away], wg.at[0, 0, 0, c], dev(other=True))
    cc = [send(cs.at[0], cr.at[0], dev(other=True))]
    w3, w4, w5 = {}, {}, ([], [])

    groups = (slice(0, 1), slice(1, 3), slice(3, 4))

    def spread_y(k):
        part = wg.at[0, 0, groups[k], 1 - yl]
        w3[k] = send(part, wg.at[0, 1, groups[k], 1 - yl], dev(jy=3))

    def spread_z(k):
        for core, dz in ((0, 1), (1, -1)):
            part = wg.at[0, 0, groups[k], core]
            w5[0].append(send(part, wg.at[1, 0, groups[k], core], dev(dz=dz)))

    def share(k):
        w3[k].wait_recv()
        part = wg.at[0, 1, groups[k], yl]
        w4[k] = send(part, wg.at[0, 1, groups[k], yl], dev(jy=1))
        w5[1].append(send(part, wg.at[1, 1, groups[k], yl], dev(dz=1 - 2 * yl)))

    def pass_on(k):
        w4[k].wait_recv()
        part = wg.at[0, 1, groups[k], 1 - yl]
        w5[1].append(send(part, wg.at[1, 1, groups[k], 1 - yl], dev(dz=2 * yl - 1)))

    c_copies = {}
    r1_copies = {}

    def for_sibling(jx):
        if jx != 2:
            sibling_terms(jx)
        for jyh in (1, 0):
            c_copies[jx, jyh] = send(c_send.at[jx, jyh], c_recv.at[jx, jyh], dev(other=True))

    def own(jx):
        for jyh in (1, 0):
            piece = term(jx, jyh, c)
            c_copies[jx, jyh].wait_recv()
            for b in range(4):
                for jl in range(2):
                    jy = jyh * 2 + jl
                    total = (piece(b, jl) + c_recv[jx, jyh, b, jl].astype(F32)).astype(BF16)
                    if b < 2:
                        s_buf[b, jx, jy] = total
                    else:
                        s_buf[b, jy, jx] = total
            pair = slice(jyh * 2, jyh * 2 + 2)
            for b, (axis, m1, m2) in enumerate(ROUTES):
                low = min(m1, 2)
                if axis == "x" and jx in (m1, 2):
                    r1_copies[b, jx, jyh] = send(
                        s_buf.at[b, jx, pair], r1.at[b, jx - low, pair], dev(jx=m1)
                    )
        for b, (axis, m1, m2) in enumerate(ROUTES):
            low = min(m1, 2)
            if axis == "y":
                r1_copies[b, jx] = send(
                    s_buf.at[b, low:low + 2, jx], r1.at[b, :, jx], dev(jy=m1)
                )

    for_sibling(2)
    for_sibling(1)
    own(2)
    for_sibling(3)
    own(1)
    cc[0].wait_recv()
    cs[1] = cs[0] + cr[0]
    cc.append(send(cs.at[1], cr.at[1], dev(jx=1)))
    for_sibling(0)
    own(3)
    own(0)
    w0.wait_recv()
    w1a = send(wg.at[0, 0, 0], wg.at[0, 0, 1], dev(jx=1))
    w1b = send(wg.at[0, 0, 0], wg.at[0, 0, 2], dev(jx=3))
    spread_y(0)
    spread_z(0)

    ld_low.wait()
    ld_gain.wait()
    gain = gain_v[...]

    def norm_rows(i, carry):
        rows = pl.ds(pl.multiple_of(i * 16, 16), 16)
        v = low_v[0, rows, :].astype(F32)
        mean_sq = jnp.sum(v * v, axis=1, keepdims=True) * (1.0 / 4096)
        normed[rows, :] = (v * lax.rsqrt(mean_sq + EPS) * gain).astype(BF16)
        return carry

    lax.fori_loop(0, 2, norm_rows, 0)

    def to(axis, mask):
        return dev(jx=mask) if axis == "x" else dev(jy=mask)

    r2_copies = {}
    for jx in ORDER:
        for b, (axis, m1, m2) in enumerate(ROUTES):
            low = min(m1, 2)
            if axis == "x":
                if jx not in (m1, 2):
                    continue
                slot = m2 if jx == 2 else 0
                for jyh in (1, 0):
                    pair = slice(jyh * 2, jyh * 2 + 2)
                    r1_copies[b, jx, jyh].wait_recv()
                    s_buf[b, slot, pair] = s_buf[b, slot, pair] + r1[b, jx - low, pair]
                    if slot:
                        r2_copies[b, jyh] = send(
                            s_buf.at[b, m2, pair], r2.at[b, pair], to(axis, m2)
                        )
            else:
                r1_copies[b, jx].wait_recv()
                s_buf[b, m2, jx] = s_buf[b, m2, jx] + r1[b, 2 - low, jx]
                r2_copies[b, jx] = send(s_buf.at[b, m2, jx], r2.at[b, jx], to(axis, m2))
                s_buf[b, 0, jx] = s_buf[b, 0, jx] + r1[b, m1 - low, jx]

    cc[1].wait_recv()
    cs[2] = cs[1] + cr[1]
    cc.append(send(cs.at[2], cr.at[2], dev(jx=3)))
    pl.semaphore_wait(far_sem.at[0], 2)
    far_signal(1)
    lax.fori_loop(2, 5, norm_rows, 0)

    r3_copies = {}

    def forward(b, s, other, m1):
        s_buf[b, 0, s] = s_buf[b, 0, s] + r2[b, s]
        if s in (m1, 2):
            r3_copies[b, s] = send(s_buf.at[b, 0, s], r3.at[b, s - min(m1, 2)], to(other, m1))

    for jx in ORDER:
        for b, (axis, m1, m2) in enumerate(ROUTES):
            if axis == "y":
                r2_copies[b, jx].wait_recv()
                forward(b, jx, "x", m1)
            elif jx in (2, 1):
                jyh = jx - 1
                r2_copies[b, jyh].wait_recv()
                for s in (2, 3) if jyh else (1, 0):
                    forward(b, s, "y", m1)

    cc[2].wait_recv()
    cs[3] = cs[2] + cr[2]
    cc.append(send(cs.at[3], cr.at[3], dev(jy=2)))
    lax.fori_loop(5, 8, norm_rows, 0)
    nb = send(normed.at[0:128], normed.at[128:256], dev(other=True))


    w1a.wait_recv()
    w1b.wait_recv()
    w2a = send(wg.at[0, 0, 2, 0], wg.at[0, 0, 3, 0], dev(jx=1))
    w2b = send(wg.at[0, 0, 1, 1], wg.at[0, 0, 3, 1], dev(jx=3))
    spread_y(1)
    spread_z(1)
    share(0)

    r4_copies = []
    for b, (axis, m1, m2) in enumerate(ROUTES):
        other = "y" if axis == "x" else "x"
        low = min(m1, 2)
        r3_copies[b, 2].wait_recv()
        s_buf[b, 0, m2] = s_buf[b, 0, m2] + r3[b, 2 - low]
        r4_copies.append(send(s_buf.at[b, 0, m2], r4.at[b], to(other, m2)))
        r3_copies[b, m1].wait_recv()
        s_buf[b, 0, 0] = s_buf[b, 0, 0] + r3[b, m1 - low]

    pl.semaphore_wait(far_sem.at[1], 2)
    far_signal(2)

    z1_copies = []
    for b in (1, 2, 3):
        r4_copies[b].wait_recv()
        s_buf[b, 0, 0] = s_buf[b, 0, 0] + r4[b]
        z1_copies.append(send(s_buf.at[b, 0, 0], z1.at[b - 1], dev(dz=(0, 1, 2, -1)[b])))
    r4_copies[0].wait_recv()
    kept = s_buf[0, 0, 0].astype(F32) + r4[0].astype(F32)
    pass_on(0)

    cc[3].wait_recv()
    counts = (cs[3] + cr[3])[0:1]
    start = jnp.sum(jnp.where(lane_f == id_col, counts, 0.0), axis=1, keepdims=True)
    first_token = (node * 128).astype(F32)
    token = lax.broadcasted_iota(jnp.int32, (128, 1), 0).astype(F32)
    positions = token + first_token - start
    ld_freq.wait()
    angle = positions * freq_v[...]
    trig[0] = jnp.cos(angle)
    trig[1] = jnp.where(lane < 64, -1.0, 1.0) * jnp.sin(angle)


    def project(jp, jyh):
        for slot, jx in enumerate((0, 1, 3, 2)):
            owner = (yh + jyh - 2 * yh * jyh) * 8 + flip(x, jx) * 2
            half = par if jp == 0 else 1 - par
            lhs = jnp.concatenate(
                [
                    normed[:, pl.ds(pl.multiple_of((owner + s) * 256 + half * 128, 128), 128)]
                    for s in range(2)
                ],
                axis=1,
            )
            part = jnp.dot(lhs, wg[jp, jyh, slot].reshape(256, 256), preferred_element_type=F32)
            if jp == 0 and jyh == 0 and jx == 0:
                acc[...] = part
            else:
                acc[...] += part

    w2a.wait_recv()
    w2b.wait_recv()
    spread_y(2)
    spread_z(2)
    share(1)
    nb.wait_recv()
    project(0, 0)

    for copy in z1_copies:
        copy.wait_recv()
    kept = kept + z1[0].astype(F32) + z1[1].astype(F32)
    late = z1[2].astype(F32)
    kept = kept + jnp.concatenate([late[7:8], late[0:7]], axis=0)
    zs[...] = kept.astype(BF16)
    pl.semaphore_wait(far_sem.at[2], 2)
    z2_copies = {a: send(zs.at[a], z2.at[a - 1], dev(dz=4 * a)) for a in (4, 3, 5, 2, 6, 1, 7)}

    share(2)
    pass_on(1)
    pass_on(2)
    project(0, 1)
    for jyh in range(2):
        for copy in w5[jyh]:
            copy.wait_recv()
        project(1, jyh)
    kx = send(acc.at[128:256], kr, dev(other=True))

    def rotate(source, half):
        for h in range(2):
            k = source[0:128, h * 128:(h + 1) * 128]
            turned = k * trig[0] + pltpu.roll(k, 64, 1) * trig[1]
            lanes = pl.ds(pl.multiple_of(half * 256 + h * 128, 128), 128)
            keys_ref[:, lanes] = turned.astype(BF16)

    rotate(acc, c)
    kx.wait_recv()
    rotate(kr, 1 - c)

    total = kept[0]
    for a in range(1, 8):
        z2_copies[a].wait_recv()
        total = total + z2[a - 1].astype(F32)
    grad_ref[...] = total

    for copy in sent:
        copy.wait_send()


def fused(x_this, grad_values, x_lower, gain, weight_lower, ids, freq):
    tiles = (8, 16, 128)
    anywhere = pl.BlockSpec(memory_space=pl.ANY)
    vmem = pl.BlockSpec(memory_space=pltpu.VMEM)
    return pl.pallas_call(
        kernel,
        out_shape=(
            pltpu.VMEM((16, 128), F32),
            pltpu.VMEM((128, 512), BF16),
        ),
        in_specs=[anywhere] * 7,
        out_specs=(vmem, vmem),
        scratch_shapes=[
            pltpu.VMEM((1, 128, 4096), BF16),
            pltpu.VMEM((1, 128, 512), BF16),
            pltpu.VMEM((1, 128, 4096), BF16),
            pltpu.VMEM((1, 4096), F32),
            pltpu.VMEM((256, 512), BF16),
            pltpu.VMEM((1, 128), jnp.int32),
            pltpu.VMEM((1, 128), F32),
            pltpu.VMEM((32, 2, 8, 128), F32),
            pltpu.VMEM((1024, 128), BF16),
            pltpu.VMEM((4, 2, 4, 2) + tiles, BF16),
            pltpu.VMEM((4, 2, 4, 2) + tiles, BF16),
            pltpu.VMEM((4, 4, 4) + tiles, BF16),
            pltpu.VMEM((4, 2, 4) + tiles, BF16),
            pltpu.VMEM((4, 4) + tiles, BF16),
            pltpu.VMEM((4, 2) + tiles, BF16),
            pltpu.VMEM((4,) + tiles, BF16),
            pltpu.VMEM((3,) + tiles, BF16),
            pltpu.VMEM((7, 16, 128), BF16),
            pltpu.VMEM(tiles, BF16),
            pltpu.VMEM((2, 2, 4, 2, 128, 256), BF16),
            pltpu.VMEM((256, 4096), BF16),
            pltpu.VMEM((256, 256), F32),
            pltpu.VMEM((128, 256), F32),
            pltpu.VMEM((4, 8, 128), F32),
            pltpu.VMEM((4, 8, 128), F32),
            pltpu.VMEM((2, 128, 128), F32),
            pltpu.SemaphoreType.DMA((7,)),
            pltpu.SemaphoreType.DMA((N_SEM,)),
            pltpu.SemaphoreType.DMA((N_SEM,)),
            pltpu.SemaphoreType.REGULAR((3,)),
        ],
        compiler_params=pltpu.CompilerParams(
            collective_id=0, has_side_effects=True, vmem_limit_bytes=60 * 1024 * 1024
        ),
        cost_estimate=pl.CostEstimate(
            flops=2 * 2 * 128 * 4096 * 512, bytes_accessed=4 * 1024 * 1024, transcendentals=32768
        ),
    )(x_this, grad_values, x_lower, gain, weight_lower, ids, freq)


def on_device(x_this, grad_values, x_lower, norm_gain, weight_lower, segment_ids):
    exponent = np.arange(128) % 64 * 2.0 / 128
    freq = jnp.asarray((500000.0 ** (-exponent)).astype(np.float32)[None])
    grad, keys = fused(
        x_this, grad_values, x_lower, norm_gain[None], weight_lower, segment_ids, freq
    )
    grad = grad.reshape(2, 8, 128).transpose(0, 2, 1).reshape(256, 8)
    return (grad, keys[None])


def solution(mesh):
    return jax.shard_map(
        on_device,
        mesh=mesh,
        in_specs=(
            P("dp", "node", None),
            P("dp", "node", None),
            P("dp", "node", None),
            P(),
            P("node", None),
            P("dp", "node"),
        ),
        out_specs=(P("node", "dp"), P("dp", "node", None)),
        check_vma=False,
    )
```
